512 devices in a mesh: group: 16 (over y, core), owner: 32 (over z, x).
Axes of the slice: x: 4, y: 8, z: 8, core: 2. Of those that a mesh axis runs over, the one named last changes fastest.
Arguments:
- embeddings: bfloat16 [65536, 1024], P('owner'), may hold values from -250 to 250
- cluster_of: int32 [65536], P('owner'), may hold values from 0 to 31, as said below
- cluster_owner: int32 [32], replicated, may hold values from 0 to 31, as said below
- slot_of: int32 [65536], P('owner'), may hold values from 0 to 2047, as said below
- pairs: int32 [32, 16, 49, 2], P('owner', 'group'), may hold values from -1 to 47, as said below
Outputs:
- similarity_max: float32 [32, 2048], P('owner', 'group')
The draws below stay inside these ranges and needn't reach their ends.
Inputs may be any that keep to these rules, and one draw needn't show every extreme that they name: `cluster_owner`: each owner owns exactly one cluster. `cluster_of`: the rows of one index of owner go to one owner in 96 rows, to another in 32 rows and to each other owner in 64 rows; every owner receives exactly 2048 rows. `slot_of`: rows with the same owner have distinct slots. `pairs`: an entry (i, j) names block i of the owner's 16 blocks (slot order) and block j of the owner's wide rows: j < 16 is the previous owner's block j, 16 <= j < 32 its own block j - 16 with i <= j - 16, higher j the next owner's block j - 2 * 16 (owners cyclic). Valid entries stand first in each list, the rest are -1 in both places. No pair is listed twice among one owner's lists. Owner o lists (i, 32 + j) exactly when owner o + 1 lists (j, i). In every owner, a quarter of the indices of group hold 49 valid entries each, and the others share the remaining ones as evenly as possible.
All inputs are finite; a program needn't handle non-finite values.
Results may differ from the reference program's by a relative error of at most 0.00049.
Values may be sent and summed in bfloat16 or wider, within the bound.
No kernel may reach another device: no remote copies, remote signals or barrier semaphores. Data moves between devices by JAX's collectives and lax.ppermute only.
A program may use at most 128 MiB of HBM per device.

```python
import jax
import jax.numpy as jnp
import numpy as np
from jax import lax

D = 1024
BLOCK = 128
ROW_DEV = 2048
TILES = 392
LIST = 49
N_GROUP = 16
N_OWNER = 32


def layout_tables(key):
    key_order, key_rows, key_slots, key_labels = jax.random.split(key, 4)
    owner_ids = jnp.arange(N_OWNER, dtype=jnp.int32)
    base_count = ROW_DEV // N_OWNER
    half_count = base_count // 2
    chosen = jax.random.permutation(key_order, N_OWNER).astype(jnp.int32)
    chosen_next = jnp.roll(chosen, -1)
    counts = base_count + half_count * (owner_ids[None, :] == chosen[:, None]).astype(jnp.int32) - half_count * (owner_ids[None, :] == chosen_next[:, None]).astype(jnp.int32)
    count_ends = jnp.cumsum(counts, axis=1)
    places = jnp.arange(ROW_DEV, dtype=jnp.int32)
    sorted_owner = jnp.sum((count_ends[:, None, :] <= places[None, :, None]).astype(jnp.int32), axis=2)
    row_keys = jax.random.split(key_rows, N_OWNER)
    row_owner = jax.vmap(jax.random.permutation)(row_keys, sorted_owner)
    flat_owner = row_owner.reshape(-1).astype(jnp.int32)
    onehot = (flat_owner[:, None] == owner_ids[None, :]).astype(jnp.int32)
    arrival = jnp.sum((jnp.cumsum(onehot, axis=0) - onehot) * onehot, axis=1)
    slot_keys = jax.random.split(key_slots, N_OWNER)
    slot_table = jax.vmap(lambda sub_key: jax.random.permutation(sub_key, ROW_DEV))(slot_keys).astype(jnp.int32)
    row_slot = slot_table[flat_owner, arrival].astype(jnp.int32)
    label_owner = jax.random.permutation(key_labels, N_OWNER).astype(jnp.int32)
    owner_label = jnp.argsort(label_owner).astype(jnp.int32)
    row_cluster = owner_label[flat_owner].astype(jnp.int32)
    return (flat_owner, row_slot, label_owner, row_cluster)


def draw_cluster_of(key, part):
    tables = layout_tables(key)
    return tables[3]


def draw_cluster_owner(key, part):
    tables = layout_tables(key)
    return tables[2]


def draw_slot_of(key, part):
    tables = layout_tables(key)
    return tables[1]


def draw_embeddings(key, part):
    tables = layout_tables(key)
    key = jax.random.fold_in(key, 5)
    flat_owner = tables[0]
    row_slot = tables[1]
    keys = jax.random.split(key, 6)
    total_rows = N_OWNER * ROW_DEV
    shared = jnp.clip(jax.random.normal(keys[0], (N_OWNER, D), jnp.float32), -5.0, 5.0)
    centre = (shared + jnp.roll(shared, -1, axis=0)) * 0.7071
    weight_lead = jax.random.uniform(keys[1], (total_rows, 1), jnp.float32, 0.2, 0.6)
    noise = jnp.clip(jax.random.normal(keys[2], (total_rows, D), jnp.float32), -5.0, 5.0)
    owner_line = jnp.arange(total_rows, dtype=jnp.int32) // ROW_DEV
    base_rows = weight_lead * centre[owner_line] + noise
    partner_kind = jax.random.randint(keys[3], (total_rows,), 0, 4)
    partner_slot = jax.random.randint(keys[4], (total_rows,), 0, ROW_DEV)
    owner_step = jnp.where(partner_kind == 2, -1, jnp.where(partner_kind == 3, 1, 0))
    partner = (owner_line + owner_step + N_OWNER) % N_OWNER * ROW_DEV + partner_slot
    mixing = jax.random.uniform(keys[5], (total_rows, 1), jnp.float32, 0.3, 1.5)
    mixed = base_rows + mixing * base_rows[partner]
    shard_rows = mixed[flat_owner * ROW_DEV + row_slot]
    return shard_rows.astype(jnp.bfloat16)


def owner_lists(cross, previous, order_key, rank_key):
    block_count = ROW_DEV // BLOCK
    upper_first, upper_second = np.triu_indices(block_count)
    grid_first = jnp.asarray(np.repeat(np.arange(block_count), block_count), jnp.int32)
    grid_second = jnp.asarray(np.tile(np.arange(block_count), block_count), jnp.int32)
    own_list = jnp.asarray(np.stack([upper_first, upper_second + block_count], axis=1), jnp.int32)
    half_pairs = block_count * block_count // 2
    next_pick = jnp.argsort(1 - cross.reshape(-1), stable=True)[:half_pairs]
    next_list = jnp.stack([grid_first[next_pick], grid_second[next_pick] + 2 * block_count], axis=1)
    prev_pick = jnp.argsort(1 - previous.T.reshape(-1), stable=True)[:half_pairs]
    prev_list = jnp.stack([grid_first[prev_pick], grid_second[prev_pick]], axis=1)
    listed = jnp.concatenate([own_list, next_list, prev_list], axis=0).astype(jnp.int32)
    listed = jax.random.permutation(order_key, listed, axis=0)
    group_rank = jax.random.permutation(rank_key, N_GROUP).astype(jnp.int32)
    high_count = N_GROUP // 4
    low_groups = N_GROUP - high_count
    remaining = TILES - high_count * LIST
    low_index = group_rank - high_count
    counts = jnp.where(group_rank < high_count, LIST, remaining // low_groups + (low_index < remaining % low_groups).astype(jnp.int32))
    starts = jnp.cumsum(counts) - counts
    places = jnp.arange(LIST, dtype=jnp.int32)
    slot_index = jnp.clip(starts[:, None] + places[None, :], 0, TILES - 1)
    filled = places[None, :] < counts[:, None]
    picked = listed[slot_index]
    return jnp.where(filled[:, :, None], picked, -1).astype(jnp.int32)


def draw_pairs(key, part):
    key = jax.random.fold_in(key, 9)
    block_count = ROW_DEV // BLOCK
    cross_key, order_key, rank_key = jax.random.split(key, 3)
    row_keys = jax.random.split(cross_key, N_OWNER * block_count)
    shuffled = jax.vmap(lambda sub_key: jax.random.permutation(sub_key, block_count))(row_keys)
    cross = (shuffled < block_count // 2).astype(jnp.int32).reshape(N_OWNER, block_count, block_count)
    previous = jnp.roll(cross, 1, axis=0)
    order_keys = jax.random.split(order_key, N_OWNER)
    rank_keys = jax.random.split(rank_key, N_OWNER)
    return jax.vmap(owner_lists)(cross, previous, order_keys, rank_keys)


def setup_inputs(seed: int = 0) -> dict:
    seeds = jax.random.split(jax.random.key(seed), 6)
    return {
        "embeddings": draw_embeddings(jax.random.fold_in(seeds[5], 71), 0),
        "cluster_of": draw_cluster_of(jax.random.fold_in(seeds[5], 71), 0),
        "cluster_owner": draw_cluster_owner(jax.random.fold_in(seeds[5], 71), 0),
        "slot_of": draw_slot_of(jax.random.fold_in(seeds[5], 71), 0),
        "pairs": draw_pairs(jax.random.fold_in(seeds[5], 71), 0),
    }


def block_mask(entries, block_count):
    first_block = entries[:, 0]
    second = entries[:, 1]
    valid = first_block >= 0
    paired = jnp.zeros((block_count, 3 * block_count), jnp.int32)
    row_pick = jnp.where(valid, first_block, block_count).astype(jnp.int32)
    col_pick = jnp.where(valid, second, 0).astype(jnp.int32)
    paired = paired.at[row_pick, col_pick].max(1, mode='drop')
    middle = second - block_count
    mirror = jnp.logical_and(valid, jnp.logical_and(middle >= 0, middle < block_count))
    mirror_row = jnp.where(mirror, middle, block_count).astype(jnp.int32)
    mirror_col = jnp.where(mirror, first_block + block_count, 0).astype(jnp.int32)
    return paired.at[mirror_row, mirror_col].max(1, mode='drop')

def reference(embeddings, cluster_of, cluster_owner, slot_of, pairs):
    owner_of = cluster_owner[cluster_of].astype(jnp.int32)
    flat_index = (owner_of * ROW_DEV + slot_of).astype(jnp.int32)
    placed = jnp.zeros((N_OWNER * ROW_DEV, D), jnp.bfloat16).at[flat_index].set(embeddings)
    floats = placed.astype(jnp.float32)
    unit_rows = (floats * lax.rsqrt(lax.optimization_barrier(jnp.sum(floats * floats, axis=1, keepdims=True)) + 1e-06)).astype(jnp.bfloat16)
    unit_rows = unit_rows.reshape(N_OWNER, ROW_DEV, D)
    block_count = ROW_DEV // BLOCK
    row_blocks = jnp.arange(ROW_DEV, dtype=jnp.int32) // BLOCK
    wide_blocks = jnp.arange(3 * ROW_DEV, dtype=jnp.int32) // BLOCK
    self_pair = jnp.arange(3 * ROW_DEV, dtype=jnp.int32)[None, :] == jnp.arange(ROW_DEV, dtype=jnp.int32)[:, None] + ROW_DEV

    def per_owner(owner_index):
        own_rows = unit_rows[owner_index]
        earlier = unit_rows[(owner_index + N_OWNER - 1) % N_OWNER]
        later_rows = unit_rows[(owner_index + 1) % N_OWNER]
        wide_rows = jnp.concatenate([earlier, own_rows, later_rows], axis=0)
        paired = block_mask(pairs[owner_index].reshape(-1, 2), block_count)
        allowed = paired[row_blocks][:, wide_blocks] > 0
        allowed = jnp.logical_and(allowed, jnp.logical_not(self_pair))
        scores = jnp.dot(own_rows.astype(jnp.float32), wide_rows.astype(jnp.float32).T, preferred_element_type=jnp.float32)
        return lax.optimization_barrier(jnp.max(jnp.where(allowed, scores, jnp.float32(-2.0)), axis=1))
    return lax.map(per_owner, jnp.arange(N_OWNER, dtype=jnp.int32))
```

```python
import jax
import jax.numpy as jnp
from jax import lax
from jax.experimental import pallas as pl
from jax.experimental.pallas import tpu as pltpu
from jax.sharding import PartitionSpec as P

BLOCK = 128
LANES = 128
META = 8
PAY_META = 16
BF16 = jnp.bfloat16
F32 = jnp.float32
I32 = jnp.int32


def iota(shape, dim):
    return lax.broadcasted_iota(I32, shape, dim)


def ones_where(mask):
    return jnp.where(mask, 1.0, 0.0).astype(BF16)


def mm(a, b):
    return jnp.dot(a, b, preferred_element_type=F32)


def mm_nt(a, b):
    return lax.dot_general(a, b, (((1,), (1,)), ((), ())), preferred_element_type=F32)


def mm_tn(a, b):
    return lax.dot_general(a, b, (((0,), (0,)), ((), ())), preferred_element_type=F32)


def send_kernel(n_owner, n_group, cap, pieces, me_ref, cluster_ref, owner_ref, slot_ref, emb_ref, out_ref, emb, wide, sems):
    rows, feat = emb.shape
    chunks = feat // LANES
    step = rows // pieces
    copies = [
        pltpu.make_async_copy(emb_ref.at[pl.ds(i * step, step)], emb.at[pl.ds(i * step, step)], sems.at[i])
        for i in range(pieces)
    ]
    for copy in copies:
        copy.start()
    me = me_ref[0]
    picked = ones_where(iota((n_owner, rows), 0) == cluster_ref[...])
    table = ones_where(iota((n_owner, n_owner), 0) == owner_ref[...])
    to = mm(table, picked).astype(BF16)
    parts = rows // LANES
    stacked = jnp.concatenate([to[:, i * LANES : (i + 1) * LANES] for i in range(parts)], axis=0)
    before = mm(stacked, ones_where(iota((LANES, LANES), 0) < iota((LANES, LANES), 1)))
    totals = mm(stacked, jnp.ones((LANES, LANES), BF16))
    running = jnp.zeros((n_owner, LANES), F32)
    lane_owner = iota((n_owner, LANES), 0).astype(F32)
    place, target = [], []
    for i in range(parts):
        here = stacked[i * n_owner : (i + 1) * n_owner].astype(F32)
        spot = before[i * n_owner : (i + 1) * n_owner] + running
        place.append(jnp.sum(here * spot, axis=0, keepdims=True))
        target.append(jnp.sum(here * lane_owner, axis=0, keepdims=True))
        running = running + totals[i * n_owner : (i + 1) * n_owner]
    place = jnp.concatenate(place, axis=1).astype(I32)
    target = jnp.concatenate(target, axis=1).astype(I32)
    mine = (place & (n_group - 1)) == me
    entry = place // n_group
    goal = jnp.where(mine, target * cap + entry, -1)
    slot = slot_ref[...]
    high = (slot // BLOCK + 1).astype(F32)
    low = (slot & (BLOCK - 1)).astype(F32)
    at_entry = jnp.logical_and(iota((LANES, rows), 0) == entry, mine)
    meta_high = mm_nt(to, jnp.where(at_entry, high, 0.0).astype(BF16)).astype(BF16)
    meta_low = mm_nt(to, jnp.where(at_entry, low, 0.0).astype(BF16)).astype(BF16)
    line = iota((n_owner * META, n_owner), 0)
    peer = iota((n_owner * META, n_owner), 1)
    meta = mm(ones_where(line == peer * META), meta_high) + mm(ones_where(line == peer * META + 1), meta_low)
    out_ref[:, cap * chunks :, :] = meta.reshape(n_owner, META, LANES).astype(BF16)
    select = ones_where(iota((n_owner * cap, rows), 0) == goal)
    total = None
    for i, copy in enumerate(copies):
        copy.wait()
        part = mm(select[:, i * step : (i + 1) * step], emb[pl.ds(i * step, step), :])
        total = part if total is None else total + part
    for k in range(chunks):
        wide[pl.ds(k, n_owner * cap, chunks), :] = total[:, k * LANES : (k + 1) * LANES]
    out_ref[:, : cap * chunks, :] = wide[...].reshape(n_owner, cap * chunks, LANES).astype(BF16)


def receive_kernel(n_owner, cap, feat, in_ref, first_ref, second_ref, out_ref, wide):
    chunks = feat // LANES
    lines = n_owner * cap
    wide[...] = in_ref[:, : cap * chunks, :].astype(F32).reshape(lines * chunks, LANES)
    meta = in_ref[:, cap * chunks :, :].astype(F32).reshape(n_owner * META, LANES).astype(BF16)
    line = iota((lines, n_owner * META), 0)
    source = iota((lines, n_owner * META), 1)
    at_lane = iota((lines, LANES), 1) == lax.rem(iota((lines, LANES), 0), cap)
    high = mm(ones_where(source == line // cap * META), meta)
    low = mm(ones_where(source == line // cap * META + 1), meta)
    ones = jnp.ones((LANES, LANES), BF16)
    high = mm(jnp.where(at_lane, high, 0.0).astype(BF16), ones)
    low = mm(jnp.where(at_lane, low, 0.0).astype(BF16), ones)
    valid = ones_where(high > 0.5)
    earlier = ones_where(iota((lines, lines), 1) < iota((lines, lines), 0))
    place = mm(earlier, valid)
    put = jnp.logical_and(place == iota((lines, BLOCK), 1).astype(F32), high > 0.5)
    put_one = ones_where(put)
    parts = []
    square = None
    for k in range(chunks):
        part = mm_tn(put_one, wide[pl.ds(k, lines, chunks), :].astype(BF16))
        parts.append(part)
        here = part * part
        square = here if square is None else square + here
    scale = lax.rsqrt(jnp.sum(square, axis=1, keepdims=True) + 1e-06)
    for k in range(chunks):
        out_ref[pl.ds(k * BLOCK, BLOCK), :] = (parts[k] * scale).astype(BF16)
    blocks = jnp.sum(jnp.where(put, high, 0.0), axis=0, keepdims=True) - 1.0
    inner = jnp.sum(jnp.where(put, low, 0.0), axis=0, keepdims=True)
    row = iota((PAY_META, LANES), 0)
    numbers = jnp.where(row == 0, blocks, jnp.where(row == 1, inner, 0.0))
    numbers = jnp.where(row == 2, first_ref[...].astype(F32), numbers)
    numbers = jnp.where(row == 3, second_ref[...].astype(F32), numbers)
    out_ref[pl.ds(chunks * BLOCK, PAY_META), :] = numbers.astype(BF16)


def rows_of(ref, start, chunks):
    return jnp.concatenate(
        [ref[pl.ds(start + k * BLOCK, BLOCK), :] for k in range(chunks)], axis=1
    )


def score_kernel(n_group, feat, me_ref, all_ref, own_ref, low_ref, high_ref, out_ref):
    chunks = feat // LANES
    size = feat + PAY_META
    blocks = n_group
    me = me_ref[0]
    numbers = [all_ref[pl.ds(b * size + feat, PAY_META), :].astype(F32) for b in range(blocks)]

    def numbers_row(i):
        return jnp.concatenate([n[i : i + 1, :] for n in numbers], axis=1).astype(I32)

    block_of, inner_of = numbers_row(0), numbers_row(1)
    first, second = numbers_row(2), numbers_row(3)
    total = blocks * LANES
    first_rows = iota((blocks, total), 0)
    wide_rows = iota((3 * blocks, total), 0)
    paired = mm_nt(ones_where(wide_rows == second), ones_where(first_rows == first))
    paired += mm_nt(ones_where(wide_rows == first + blocks), ones_where(first_rows == second - blocks))
    penalty = jnp.where(paired > 0.5, 0.0, -4.0).astype(BF16)
    sources = [low_ref, own_ref, high_ref]
    marks = [r[pl.ds(feat, PAY_META), :].astype(F32)[0:1, :].astype(I32) + n * blocks for n, r in enumerate(sources)]
    marks = jnp.concatenate(marks, axis=1)
    source_one = ones_where(iota((3 * blocks, 3 * BLOCK), 0) == marks)
    bias = mm_tn(source_one, penalty).astype(BF16)
    left = jnp.concatenate([rows_of(r, 0, chunks) for r in sources], axis=0)
    best = []
    pair = 2 * BLOCK
    for b in range(blocks // 2):
        right = jnp.concatenate([rows_of(all_ref, (2 * b + h) * size, chunks) for h in range(2)], axis=0)
        here = ones_where(iota((blocks, pair), 0) == block_of[:, b * pair : (b + 1) * pair])
        scores = mm_nt(left, right) + mm(bias, here)
        own = scores[BLOCK : 2 * BLOCK]
        same = iota((BLOCK, pair), 1) + b * pair == iota((BLOCK, pair), 0) + me * BLOCK
        own = jnp.where(same, -2.0, own)
        top = jnp.maximum(jnp.maximum(scores[:BLOCK], own), scores[2 * BLOCK :])
        best.append(jnp.max(top, axis=0, keepdims=True))
    best = jnp.maximum(jnp.concatenate(best, axis=1), -2.0)
    spread = iota((blocks, total), 0) == block_of
    inner = ones_where(iota((BLOCK, total), 0) == inner_of)
    result = jnp.zeros((blocks, BLOCK), F32)
    rest = best
    for _ in range(3):
        piece = rest.astype(BF16).astype(F32)
        rest = rest - piece
        result += mm_nt(jnp.where(spread, piece, 0.0).astype(BF16), inner)
    out_ref[...] = result


def vmem():
    return pl.BlockSpec(memory_space=pltpu.VMEM)


def smem():
    return pl.BlockSpec(memory_space=pltpu.SMEM)


PARAMS = pltpu.CompilerParams(vmem_limit_bytes=48 * 1024 * 1024)


def on_device(embeddings, cluster_of, cluster_owner, slot_of, pairs):
    n_owner = lax.axis_size("owner")
    n_group = lax.axis_size("group")
    rows, feat = embeddings.shape
    chunks = feat // LANES
    cap = 3 * rows // (2 * n_owner * n_group)
    pieces = 4
    me = lax.axis_index("group").astype(I32).reshape(1)
    lane_rows = cap * chunks + META
    outgoing = pl.pallas_call(
        lambda *refs: send_kernel(n_owner, n_group, cap, pieces, *refs),
        out_shape=jax.ShapeDtypeStruct((n_owner, lane_rows, LANES), BF16),
        in_specs=[smem(), vmem(), vmem(), vmem(), pl.BlockSpec(memory_space=pl.ANY)],
        out_specs=vmem(),
        scratch_shapes=[
            pltpu.VMEM((rows, feat), BF16),
            pltpu.VMEM((n_owner * cap * chunks, LANES), F32),
            pltpu.SemaphoreType.DMA((pieces,)),
        ],
        compiler_params=PARAMS,
        name="send_rows",
    )(me, cluster_of.reshape(1, rows), cluster_owner.reshape(1, n_owner), slot_of.reshape(1, rows), embeddings)
    arrived = lax.all_to_all(outgoing, "owner", split_axis=0, concat_axis=0, tiled=True)
    entries = pairs.reshape(-1, 2)
    listed = jnp.pad(entries.T, ((0, 0), (0, LANES - entries.shape[0])), constant_values=-1)
    payload = pl.pallas_call(
        lambda *refs: receive_kernel(n_owner, cap, feat, *refs),
        out_shape=jax.ShapeDtypeStruct((feat + PAY_META, LANES), BF16),
        in_specs=[vmem(), vmem(), vmem()],
        out_specs=vmem(),
        scratch_shapes=[pltpu.VMEM((n_owner * cap * chunks, LANES), F32)],
        compiler_params=PARAMS,
        name="unit_rows",
    )(arrived, listed[0:1], listed[1:2])
    forward = [(i, (i + 1) % n_owner) for i in range(n_owner)]
    backward = [(b, a) for a, b in forward]
    gathered = lax.all_gather(payload, "group", axis=0, tiled=True)
    low = lax.ppermute(payload, "owner", forward)
    high = lax.ppermute(payload, "owner", backward)
    table = pl.pallas_call(
        lambda *refs: score_kernel(n_group, feat, *refs),
        out_shape=jax.ShapeDtypeStruct((n_group, BLOCK), F32),
        in_specs=[smem(), vmem(), vmem(), vmem(), vmem()],
        out_specs=vmem(),
        compiler_params=PARAMS,
        name="score_rows",
    )(me, gathered, payload, low, high)
    shares = lax.all_to_all(table, "group", split_axis=0, concat_axis=0, tiled=True)
    return jnp.max(shares, axis=0, keepdims=True)


def solution(mesh):
    placed = (P("owner", None), P("owner"), P(), P("owner"), P("owner", "group", None, None))
    return jax.shard_map(
        on_device, mesh=mesh, in_specs=placed, out_specs=P("owner", "group"), check_vma=False
    )
```

```python
import jax
import jax.numpy as jnp
from jax import lax
from jax.experimental import pallas as pl
from jax.experimental.pallas import tpu as pltpu
from jax.sharding import PartitionSpec as P

BLOCK = 128
LANES = 128
META = 8
PAY_META = 16
UNITS = 2
BF16 = jnp.bfloat16
F32 = jnp.float32
I32 = jnp.int32


def iota(shape, dim):
    return lax.broadcasted_iota(I32, shape, dim)


def ones_where(mask):
    return jnp.where(mask, 1.0, 0.0).astype(BF16)


def mm(a, b):
    return jnp.dot(a, b, preferred_element_type=F32)


def mm_nt(a, b):
    return lax.dot_general(a, b, (((1,), (1,)), ((), ())), preferred_element_type=F32)


def mm_tn(a, b):
    return lax.dot_general(a, b, (((0,), (0,)), ((), ())), preferred_element_type=F32)


def send_kernel(n_owner, n_group, cap, shift, pieces, cluster_hbm, owner_hbm, slot_hbm, emb_ref, out_ref, emb, wide, cluster_ref, owner_ref, slot_ref, sems):
    rows, feat = emb.shape
    chunks = feat // LANES
    step = rows // pieces
    small = [
        pltpu.make_async_copy(source, goal, sems.at[pieces + i])
        for i, (source, goal) in enumerate(
            ((cluster_hbm, cluster_ref), (owner_hbm, owner_ref), (slot_hbm, slot_ref))
        )
    ]
    copies = [
        pltpu.make_async_copy(emb_ref.at[pl.ds(i * step, step)], emb.at[pl.ds(i * step, step)], sems.at[i])
        for i in range(pieces)
    ]
    for copy in small + copies:
        copy.start()
    for copy in small:
        copy.wait()
    me = lax.axis_index("group")
    picked = ones_where(iota((n_owner, rows), 0) == cluster_ref[...])
    table = ones_where(iota((n_owner, n_owner), 0) == owner_ref[...])
    to = mm(table, picked).astype(BF16)
    parts = rows // LANES
    stacked = jnp.concatenate([to[:, i * LANES : (i + 1) * LANES] for i in range(parts)], axis=0)
    before = mm(stacked, ones_where(iota((LANES, LANES), 0) < iota((LANES, LANES), 1)))
    totals = mm(stacked, jnp.ones((LANES, LANES), BF16))
    running = jnp.zeros((n_owner, LANES), F32)
    lane_owner = iota((n_owner, LANES), 0).astype(F32)
    place, target = [], []
    for i in range(parts):
        here = stacked[i * n_owner : (i + 1) * n_owner].astype(F32)
        spot = before[i * n_owner : (i + 1) * n_owner] + running
        place.append(jnp.sum(here * spot, axis=0, keepdims=True))
        target.append(jnp.sum(here * lane_owner, axis=0, keepdims=True))
        running = running + totals[i * n_owner : (i + 1) * n_owner]
    place = jnp.concatenate(place, axis=1).astype(I32)
    target = jnp.concatenate(target, axis=1).astype(I32)
    share = place & (n_group - 1)
    entry = place // n_group
    entry = jnp.where(share == me, entry, jnp.where(share == ((me + shift) & (n_group - 1)), entry + cap, -1))
    mine = entry >= 0
    lines = UNITS * cap
    goal = jnp.where(mine, target * lines + entry, -1)
    slot = slot_ref[...]
    high = (slot // BLOCK + 1).astype(F32)
    low = (slot & (BLOCK - 1)).astype(F32)
    at_entry = iota((LANES, rows), 0) == entry
    meta_high = mm_nt(to, jnp.where(at_entry, high, 0.0).astype(BF16)).astype(BF16)
    meta_low = mm_nt(to, jnp.where(at_entry, low, 0.0).astype(BF16)).astype(BF16)
    line = iota((n_owner * META, n_owner), 0)
    peer = iota((n_owner * META, n_owner), 1)
    meta = mm(ones_where(line == peer * META), meta_high) + mm(ones_where(line == peer * META + 1), meta_low)
    out_ref[:, lines * chunks :, :] = meta.reshape(n_owner, META, LANES).astype(BF16)
    select = ones_where(iota((n_owner * lines, rows), 0) == goal)
    total = None
    for i, copy in enumerate(copies):
        copy.wait()
        part = mm(select[:, i * step : (i + 1) * step], emb[pl.ds(i * step, step), :])
        total = part if total is None else total + part
    for k in range(chunks):
        wide[pl.ds(k, n_owner * lines, chunks), :] = total[:, k * LANES : (k + 1) * LANES]
    out_ref[:, : lines * chunks, :] = wide[...].reshape(n_owner, lines * chunks, LANES).astype(BF16)


def receive_kernel(n_owner, cap, feat, in_ref, near_ref, up_ref, down_ref, both_ref, first_ref, wide):
    chunks = feat // LANES
    per_peer = UNITS * cap
    lines = n_owner * per_peer
    size = feat + PAY_META
    wide[...] = in_ref[:, : per_peer * chunks, :].astype(F32).reshape(lines * chunks, LANES)
    meta = in_ref[:, per_peer * chunks :, :].astype(F32).reshape(n_owner * META, LANES).astype(BF16)
    line = iota((lines, n_owner * META), 0)
    source = iota((lines, n_owner * META), 1)
    at_lane = iota((lines, LANES), 1) == lax.rem(iota((lines, LANES), 0), per_peer)
    high = mm(ones_where(source == line // per_peer * META), meta)
    low = mm(ones_where(source == line // per_peer * META + 1), meta)
    ones = jnp.ones((LANES, LANES), BF16)
    high = mm(jnp.where(at_lane, high, 0.0).astype(BF16), ones)
    low = mm(jnp.where(at_lane, low, 0.0).astype(BF16), ones)
    valid = ones_where(high > 0.5)
    later, sooner = iota((lines, lines), 0), iota((lines, lines), 1)
    same = lax.rem(later, per_peer) // cap == lax.rem(sooner, per_peer) // cap
    place = mm(ones_where(jnp.logical_and(sooner < later, same)), valid)
    unit = lax.rem(iota((lines, BLOCK), 0), per_peer) // cap
    here = jnp.logical_and(place == iota((lines, BLOCK), 1).astype(F32), high > 0.5)
    puts = [jnp.logical_and(here, unit == n) for n in range(UNITS)]
    put_one = ones_where(jnp.concatenate(puts, axis=1))
    parts = []
    square = None
    for k in range(chunks):
        part = mm_tn(put_one, wide[pl.ds(k, lines, chunks), :].astype(BF16))
        parts.append(part)
        here = part * part
        square = here if square is None else square + here
    scale = lax.rsqrt(jnp.sum(square, axis=1, keepdims=True) + 1e-06)
    for k in range(chunks):
        piece = (parts[k] * scale).astype(BF16)
        for n in range(UNITS):
            both_ref[pl.ds(n * size + k * BLOCK, BLOCK), :] = piece[n * BLOCK : (n + 1) * BLOCK]
        first_ref[pl.ds(k * BLOCK, BLOCK), :] = piece[:BLOCK]
    row = iota((PAY_META, LANES), 0)
    for n in range(UNITS):
        blocks = jnp.sum(jnp.where(puts[n], high, 0.0), axis=0, keepdims=True) - 1.0
        inner = jnp.sum(jnp.where(puts[n], low, 0.0), axis=0, keepdims=True)
        numbers = jnp.where(row == 0, blocks, jnp.where(row == 1, inner, 0.0)).astype(BF16)
        both_ref[pl.ds(n * size + feat, PAY_META), :] = numbers
        if n == 0:
            first_ref[pl.ds(feat, PAY_META), :] = numbers
    lists = jnp.concatenate([near_ref[0:6, :], up_ref[0:6, :], down_ref[2:6, :]], axis=0)
    both_ref[pl.ds(UNITS * size, PAY_META), :] = lists.astype(BF16)


def rows_of(ref, start, feat):
    return jnp.concatenate([ref[pl.ds(start + k * BLOCK, BLOCK), :] for k in range(feat // LANES)], axis=1)


def numbers_of(ref, start, feat):
    return ref[pl.ds(start + feat, PAY_META), :].astype(F32)[0:2, :].astype(I32)


def stack_rows(places, feat):
    return jnp.concatenate([rows_of(ref, start, feat) for ref, start in places], axis=0)


def stack_numbers(places, feat):
    return jnp.concatenate([numbers_of(ref, start, feat) for ref, start in places], axis=1)


def best_of(left, bias, places, feat, blocks, same=None):
    right = stack_rows(places, feat)
    width = right.shape[0]
    here = ones_where(iota((blocks, width), 0) == stack_numbers(places, feat)[0:1, :])
    scores = mm_nt(left, right) + mm(bias, here)
    if same is not None:
        scores = jnp.where(same, -2.0, scores)
    return jnp.max(scores, axis=0, keepdims=True)


def bias_of(penalty, marks):
    picked = ones_where(iota((penalty.shape[0], marks.shape[1]), 0) == marks)
    return mm_tn(picked, penalty).astype(BF16)


def slot_table(best, numbers, blocks):
    total = best.shape[1]
    best = jnp.maximum(best, -2.0)
    spread = iota((blocks, total), 0) == numbers[0:1, :]
    inner = ones_where(iota((BLOCK, total), 0) == numbers[1:2, :])
    filled = mm_nt(ones_where(spread), inner)
    result = jnp.zeros((blocks, BLOCK), F32)
    rest = best
    for _ in range(3):
        piece = rest.astype(BF16).astype(F32)
        rest = rest - piece
        result += mm_nt(jnp.where(spread, piece, 0.0).astype(BF16), inner)
    return jnp.where(filled > 0.5, result, -2.0)


def first_score_kernel(blocks, feat, own_ref, twin_ref, back_ref, next_ref, low_ref, high_ref, out_ref, bias_ref):
    size = feat + PAY_META
    lists = [r[pl.ds(UNITS * size, PAY_META), :].astype(F32) for r in (own_ref, twin_ref)]
    count = PAY_META // 2

    def list_row(i):
        return jnp.concatenate([n[2 * b + i : 2 * b + i + 1, :] for n in lists for b in range(count)], axis=1).astype(I32)

    first, second = list_row(0), list_row(1)
    total = 2 * count * LANES
    first_rows = iota((blocks, total), 0)
    wide_rows = iota((3 * blocks, total), 0)
    paired = mm_nt(ones_where(wide_rows == second), ones_where(first_rows == first))
    paired += mm_nt(ones_where(wide_rows == first + blocks), ones_where(first_rows == second - blocks))
    penalty = jnp.where(paired > 0.5, 0.0, -4.0).astype(BF16)
    across = [(low_ref, 0), (low_ref, size), (high_ref, 0), (high_ref, size)]
    marks = stack_numbers(across, feat)[0:1, :]
    marks += jnp.where(iota(marks.shape, 1) < 2 * BLOCK, 0, 2 * blocks)
    across_bias = bias_of(penalty, marks)
    bias_ref[...] = across_bias
    across_rows = stack_rows(across, feat)
    inside = [(back_ref, 0), (next_ref, 0), (own_ref, 0), (twin_ref, 0), (own_ref, size), (twin_ref, size)]
    inside_bias = bias_of(penalty, stack_numbers(inside, feat)[0:1, :] + blocks)
    inside_rows = stack_rows(inside, feat)
    row, lane = iota((6 * BLOCK, 2 * BLOCK), 0), iota((6 * BLOCK, 2 * BLOCK), 1)
    same = row == lane + jnp.where(lane < BLOCK, 2 * BLOCK, 3 * BLOCK)
    groups = [
        ([(own_ref, 0), (own_ref, size)], 0, 6, same),
        ([(twin_ref, 0), (twin_ref, size)], 0, 3, None),
        ([(back_ref, 0), (next_ref, 0)], 2, 6, None),
    ]
    best, numbers = [], []
    for places, low, high, equal in groups:
        part = slice(low * BLOCK, high * BLOCK)
        one = best_of(across_rows, across_bias, places, feat, blocks)
        two = best_of(inside_rows[part], inside_bias[part], places, feat, blocks, equal)
        best.append(jnp.maximum(one, two))
        numbers.append(stack_numbers(places, feat))
    out_ref[...] = slot_table(jnp.concatenate(best, axis=1), jnp.concatenate(numbers, axis=1), blocks)


def second_score_kernel(blocks, feat, table_ref, bias_ref, low_ref, high_ref, back_ref, back_twin_ref, next_twin_ref, out_ref):
    size = feat + PAY_META
    across_rows = stack_rows([(low_ref, 0), (low_ref, size), (high_ref, 0), (high_ref, size)], feat)
    across_bias = bias_ref[...]
    best, numbers = [], []
    for places in ([(back_ref, size), (back_twin_ref, size)], [(back_twin_ref, 0), (next_twin_ref, 0)]):
        best.append(best_of(across_rows, across_bias, places, feat, blocks))
        numbers.append(stack_numbers(places, feat))
    table = slot_table(jnp.concatenate(best, axis=1), jnp.concatenate(numbers, axis=1), blocks)
    out_ref[...] = jnp.maximum(table_ref[...], table)


def vmem():
    return pl.BlockSpec(memory_space=pltpu.VMEM)


def anywhere():
    return pl.BlockSpec(memory_space=pl.ANY)


PARAMS = pltpu.CompilerParams(vmem_limit_bytes=48 * 1024 * 1024)


def cost(flops, nbytes):
    return pl.CostEstimate(flops=flops, bytes_accessed=nbytes, transcendentals=0)


def on_device(embeddings, cluster_of, cluster_owner, slot_of, pairs):
    n_owner = lax.axis_size("owner")
    n_group = lax.axis_size("group")
    rows, feat = embeddings.shape
    chunks = feat // LANES
    cap = 3 * rows // (2 * n_owner * n_group)
    lines = UNITS * cap
    pieces = 4
    size = feat + PAY_META
    outgoing = pl.pallas_call(
        lambda *refs: send_kernel(n_owner, n_group, cap, 6, pieces, *refs),
        out_shape=jax.ShapeDtypeStruct((n_owner, lines * chunks + META, LANES), BF16),
        in_specs=[anywhere()] * 4,
        out_specs=vmem(),
        scratch_shapes=[
            pltpu.VMEM((rows, feat), BF16),
            pltpu.VMEM((n_owner * lines * chunks, LANES), F32),
            pltpu.VMEM((1, rows), I32),
            pltpu.VMEM((1, n_owner), I32),
            pltpu.VMEM((1, rows), I32),
            pltpu.SemaphoreType.DMA((pieces + 3,)),
        ],
        compiler_params=PARAMS,
        name="send_rows",
    )(cluster_of.reshape(1, rows), cluster_owner.reshape(1, n_owner), slot_of.reshape(1, rows), embeddings)
    arrived = lax.all_to_all(outgoing, "owner", split_axis=0, concat_axis=0, tiled=True)
    swap = [(i, i ^ 1) for i in range(n_group)]

    def along_y(x, hops):
        return lax.ppermute(x, "group", [(i, (i + 2 * hops) % n_group) for i in range(n_group)])

    def along_owner(x, hops):
        return lax.ppermute(x, "owner", [(i, (i + hops) % n_owner) for i in range(n_owner)])

    entries = pairs.reshape(-1, 2)
    listed = jnp.pad(entries.T, ((0, 6), (0, LANES - entries.shape[0])), constant_values=-1).astype(F32)
    before, after = along_y(listed, 1), along_y(listed, -1)
    near = jnp.concatenate([before[0:2], listed[0:2], after[0:2], listed[6:8]], axis=0)
    down, up = along_y(near, 3), along_y(near, -3)
    both, first = pl.pallas_call(
        lambda *refs: receive_kernel(n_owner, cap, feat, *refs),
        out_shape=[
            jax.ShapeDtypeStruct((UNITS * size + PAY_META, LANES), BF16),
            jax.ShapeDtypeStruct((size, LANES), BF16),
        ],
        in_specs=[vmem()] * 4,
        out_specs=[vmem()] * 2,
        scratch_shapes=[pltpu.VMEM((n_owner * lines * chunks, LANES), F32)],
        compiler_params=PARAMS,
        name="unit_rows",
    )(arrived, near, up, down)
    low, high = along_owner(both, 1), along_owner(both, -1)
    back, following = along_y(both, 1), along_y(first, -1)
    twin = lax.ppermute(both, "group", swap)
    low, high, back, following, twin = lax.optimization_barrier((low, high, back, following, twin))
    back_twin, next_twin = lax.ppermute(back, "group", swap), lax.ppermute(following, "group", swap)
    table, bias = pl.pallas_call(
        lambda *refs: first_score_kernel(n_group, feat, *refs),
        out_shape=[
            jax.ShapeDtypeStruct((n_group, BLOCK), F32),
            jax.ShapeDtypeStruct((4 * BLOCK, n_group), BF16),
        ],
        in_specs=[vmem()] * 6,
        out_specs=[vmem()] * 2,
        compiler_params=PARAMS,
        cost_estimate=cost(3 * 10**9, 4 * 10**6),
        name="score_rows",
    )(both, twin, back, following, low, high)
    table = pl.pallas_call(
        lambda *refs: second_score_kernel(n_group, feat, *refs),
        out_shape=jax.ShapeDtypeStruct((n_group, BLOCK), F32),
        in_specs=[vmem()] * 7,
        out_specs=vmem(),
        compiler_params=PARAMS,
        cost_estimate=cost(5 * 10**8, 2 * 10**6),
        name="score_rest",
    )(table, bias, low, high, back, back_twin, next_twin)
    shares = lax.all_to_all(table, "group", split_axis=0, concat_axis=0, tiled=True)
    return jnp.max(shares, axis=0, keepdims=True)


def solution(mesh):
    placed = (P("owner", None), P("owner"), P(), P("owner"), P("owner", "group", None, None))
    return jax.shard_map(
        on_device, mesh=mesh, in_specs=placed, out_specs=P("owner", "group"), check_vma=False
    )
```

```python
import jax
import jax.numpy as jnp
from jax import lax
from jax.experimental import pallas as pl
from jax.experimental.pallas import tpu as pltpu
from jax.sharding import PartitionSpec as P

BLOCK = 128
LANES = 128
META = 8
PAY_META = 16
UNITS = 2
BF16 = jnp.bfloat16
F32 = jnp.float32
I32 = jnp.int32


def iota(shape, dim):
    return lax.broadcasted_iota(I32, shape, dim)


def ones_where(mask):
    return jnp.where(mask, 1.0, 0.0).astype(BF16)


def mm(a, b):
    return jnp.dot(a, b, preferred_element_type=F32)


def mm_nt(a, b):
    return lax.dot_general(a, b, (((1,), (1,)), ((), ())), preferred_element_type=F32)


def mm_tn(a, b):
    return lax.dot_general(a, b, (((0,), (0,)), ((), ())), preferred_element_type=F32)


def send_kernel(n_owner, n_group, cap, shift, pieces, cluster_hbm, owner_hbm, slot_hbm, emb_ref, out_ref, emb, wide, cluster_ref, owner_ref, slot_ref, sems):
    rows, feat = emb.shape
    chunks = feat // LANES
    step = rows // pieces
    small = [
        pltpu.make_async_copy(source, goal, sems.at[pieces + i])
        for i, (source, goal) in enumerate(
            ((cluster_hbm, cluster_ref), (owner_hbm, owner_ref), (slot_hbm, slot_ref))
        )
    ]
    copies = [
        pltpu.make_async_copy(emb_ref.at[pl.ds(i * step, step)], emb.at[pl.ds(i * step, step)], sems.at[i])
        for i in range(pieces)
    ]
    for copy in small + copies:
        copy.start()
    for copy in small:
        copy.wait()
    me = lax.axis_index("group")
    picked = ones_where(iota((n_owner, rows), 0) == cluster_ref[...])
    table = ones_where(iota((n_owner, n_owner), 0) == owner_ref[...])
    to = mm(table, picked).astype(BF16)
    parts = rows // LANES
    stacked = jnp.concatenate([to[:, i * LANES : (i + 1) * LANES] for i in range(parts)], axis=0)
    before = mm(stacked, ones_where(iota((LANES, LANES), 0) < iota((LANES, LANES), 1)))
    totals = mm(stacked, jnp.ones((LANES, LANES), BF16))
    running = jnp.zeros((n_owner, LANES), F32)
    lane_owner = iota((n_owner, LANES), 0).astype(F32)
    place, target = [], []
    for i in range(parts):
        here = stacked[i * n_owner : (i + 1) * n_owner].astype(F32)
        spot = before[i * n_owner : (i + 1) * n_owner] + running
        place.append(jnp.sum(here * spot, axis=0, keepdims=True))
        target.append(jnp.sum(here * lane_owner, axis=0, keepdims=True))
        running = running + totals[i * n_owner : (i + 1) * n_owner]
    place = jnp.concatenate(place, axis=1).astype(I32)
    target = jnp.concatenate(target, axis=1).astype(I32)
    share = place & (n_group - 1)
    entry = place // n_group
    entry = jnp.where(share == me, entry, jnp.where(share == ((me + shift) & (n_group - 1)), entry + cap, -1))
    mine = entry >= 0
    lines = UNITS * cap
    goal = jnp.where(mine, target * lines + entry, -1)
    slot = slot_ref[...]
    high = (slot // BLOCK + 1).astype(F32)
    low = (slot & (BLOCK - 1)).astype(F32)
    at_entry = iota((LANES, rows), 0) == entry
    meta_high = mm_nt(to, jnp.where(at_entry, high, 0.0).astype(BF16)).astype(BF16)
    meta_low = mm_nt(to, jnp.where(at_entry, low, 0.0).astype(BF16)).astype(BF16)
    line = iota((n_owner * META, n_owner), 0)
    peer = iota((n_owner * META, n_owner), 1)
    meta = mm(ones_where(line == peer * META), meta_high) + mm(ones_where(line == peer * META + 1), meta_low)
    out_ref[:, lines * chunks :, :] = meta.reshape(n_owner, META, LANES).astype(BF16)
    select = ones_where(iota((n_owner * lines, rows), 0) == goal)
    total = None
    for i, copy in enumerate(copies):
        copy.wait()
        part = mm(select[:, i * step : (i + 1) * step], emb[pl.ds(i * step, step), :])
        total = part if total is None else total + part
    for k in range(chunks):
        wide[pl.ds(k, n_owner * lines, chunks), :] = total[:, k * LANES : (k + 1) * LANES]
    out_ref[:, : lines * chunks, :] = wide[...].reshape(n_owner, lines * chunks, LANES).astype(BF16)


def receive_kernel(n_owner, cap, feat, in_ref, near_ref, up_ref, down_ref, both_ref, first_ref, wide):
    chunks = feat // LANES
    per_peer = UNITS * cap
    lines = n_owner * per_peer
    size = feat + PAY_META
    wide[...] = in_ref[:, : per_peer * chunks, :].astype(F32).reshape(lines * chunks, LANES)
    meta = in_ref[:, per_peer * chunks :, :].astype(F32).reshape(n_owner * META, LANES).astype(BF16)
    line = iota((lines, n_owner * META), 0)
    source = iota((lines, n_owner * META), 1)
    at_lane = iota((lines, LANES), 1) == lax.rem(iota((lines, LANES), 0), per_peer)
    high = mm(ones_where(source == line // per_peer * META), meta)
    low = mm(ones_where(source == line // per_peer * META + 1), meta)
    ones = jnp.ones((LANES, LANES), BF16)
    high = mm(jnp.where(at_lane, high, 0.0).astype(BF16), ones)
    low = mm(jnp.where(at_lane, low, 0.0).astype(BF16), ones)
    valid = ones_where(high > 0.5)
    later, sooner = iota((lines, lines), 0), iota((lines, lines), 1)
    same = lax.rem(later, per_peer) // cap == lax.rem(sooner, per_peer) // cap
    place = mm(ones_where(jnp.logical_and(sooner < later, same)), valid)
    unit = lax.rem(iota((lines, BLOCK), 0), per_peer) // cap
    here = jnp.logical_and(place == iota((lines, BLOCK), 1).astype(F32), high > 0.5)
    puts = [jnp.logical_and(here, unit == n) for n in range(UNITS)]
    put_one = ones_where(jnp.concatenate(puts, axis=1))
    parts = []
    square = None
    for k in range(chunks):
        part = mm_tn(put_one, wide[pl.ds(k, lines, chunks), :].astype(BF16))
        parts.append(part)
        here = part * part
        square = here if square is None else square + here
    scale = lax.rsqrt(jnp.sum(square, axis=1, keepdims=True) + 1e-06)
    for k in range(chunks):
        piece = (parts[k] * scale).astype(BF16)
        for n in range(UNITS):
            both_ref[pl.ds(n * size + k * BLOCK, BLOCK), :] = piece[n * BLOCK : (n + 1) * BLOCK]
        first_ref[pl.ds(k * BLOCK, BLOCK), :] = piece[:BLOCK]
    row = iota((PAY_META, LANES), 0)
    for n in range(UNITS):
        blocks = jnp.sum(jnp.where(puts[n], high, 0.0), axis=0, keepdims=True) - 1.0
        inner = jnp.sum(jnp.where(puts[n], low, 0.0), axis=0, keepdims=True)
        numbers = jnp.where(row == 0, blocks, jnp.where(row == 1, inner, 0.0)).astype(BF16)
        both_ref[pl.ds(n * size + feat, PAY_META), :] = numbers
        if n == 0:
            first_ref[pl.ds(feat, PAY_META), :] = numbers
    lists = jnp.concatenate([near_ref[0:6, :], up_ref[0:6, :], down_ref[2:6, :]], axis=0)
    both_ref[pl.ds(UNITS * size, PAY_META), :] = lists.astype(BF16)


def rows_of(ref, start, feat):
    return jnp.concatenate([ref[pl.ds(start + k * BLOCK, BLOCK), :] for k in range(feat // LANES)], axis=1)


def numbers_of(ref, start, feat):
    return ref[pl.ds(start + feat, PAY_META), :].astype(F32)[0:2, :].astype(I32)


def stack_rows(places, feat):
    return jnp.concatenate([rows_of(ref, start, feat) for ref, start in places], axis=0)


def stack_numbers(places, feat):
    return jnp.concatenate([numbers_of(ref, start, feat) for ref, start in places], axis=1)


def best_of(left, bias, places, feat, blocks, same=None):
    right = stack_rows(places, feat)
    width = right.shape[0]
    here = ones_where(iota((blocks, width), 0) == stack_numbers(places, feat)[0:1, :])
    scores = mm_nt(left, right) + mm(bias, here)
    if same is not None:
        scores = jnp.where(same, -2.0, scores)
    return jnp.max(scores, axis=0, keepdims=True)


def bias_of(penalty, marks):
    picked = ones_where(iota((penalty.shape[0], marks.shape[1]), 0) == marks)
    return mm_tn(picked, penalty).astype(BF16)


def slot_table(best, numbers, blocks):
    total = best.shape[1]
    best = jnp.maximum(best, -2.0)
    spread = iota((blocks, total), 0) == numbers[0:1, :]
    inner = ones_where(iota((BLOCK, total), 0) == numbers[1:2, :])
    filled = mm_nt(ones_where(spread), inner)
    result = jnp.zeros((blocks, BLOCK), F32)
    rest = best
    for _ in range(3):
        piece = rest.astype(BF16).astype(F32)
        rest = rest - piece
        result += mm_nt(jnp.where(spread, piece, 0.0).astype(BF16), inner)
    return jnp.where(filled > 0.5, result, -2.0)


def first_score_kernel(blocks, feat, own_ref, twin_ref, back_ref, next_ref, low_ref, high_ref, out_ref, bias_ref):
    size = feat + PAY_META
    lists = [r[pl.ds(UNITS * size, PAY_META), :].astype(F32) for r in (own_ref, twin_ref)]
    count = PAY_META // 2

    def list_row(i):
        return jnp.concatenate([n[2 * b + i : 2 * b + i + 1, :] for n in lists for b in range(count)], axis=1).astype(I32)

    first, second = list_row(0), list_row(1)
    total = 2 * count * LANES
    first_rows = iota((blocks, total), 0)
    wide_rows = iota((3 * blocks, total), 0)
    paired = mm_nt(ones_where(wide_rows == second), ones_where(first_rows == first))
    paired += mm_nt(ones_where(wide_rows == first + blocks), ones_where(first_rows == second - blocks))
    penalty = jnp.where(paired > 0.5, 0.0, -4.0).astype(BF16)
    across = [(low_ref, 0), (low_ref, size), (high_ref, 0), (high_ref, size)]
    marks = stack_numbers(across, feat)[0:1, :]
    marks += jnp.where(iota(marks.shape, 1) < 2 * BLOCK, 0, 2 * blocks)
    across_bias = bias_of(penalty, marks)
    bias_ref[...] = across_bias
    across_rows = stack_rows(across, feat)
    inside = [(back_ref, 0), (next_ref, 0), (own_ref, 0), (twin_ref, 0), (own_ref, size), (twin_ref, size)]
    inside_bias = bias_of(penalty, stack_numbers(inside, feat)[0:1, :] + blocks)
    inside_rows = stack_rows(inside, feat)
    row, lane = iota((6 * BLOCK, 2 * BLOCK), 0), iota((6 * BLOCK, 2 * BLOCK), 1)
    same = row == lane + jnp.where(lane < BLOCK, 2 * BLOCK, 3 * BLOCK)
    groups = [
        ([(own_ref, 0), (own_ref, size)], 0, 6, same),
        ([(twin_ref, 0), (twin_ref, size)], 0, 3, None),
        ([(back_ref, 0), (next_ref, 0)], 2, 6, None),
    ]
    best, numbers = [], []
    for places, low, high, equal in groups:
        part = slice(low * BLOCK, high * BLOCK)
        one = best_of(across_rows, across_bias, places, feat, blocks)
        two = best_of(inside_rows[part], inside_bias[part], places, feat, blocks, equal)
        best.append(jnp.maximum(one, two))
        numbers.append(stack_numbers(places, feat))
    out_ref[...] = slot_table(jnp.concatenate(best, axis=1), jnp.concatenate(numbers, axis=1), blocks)


def second_score_kernel(blocks, feat, table_ref, bias_ref, low_ref, high_ref, back_ref, late_ref, out_ref):
    size = feat + PAY_META
    across_rows = stack_rows([(low_ref, 0), (low_ref, size), (high_ref, 0), (high_ref, size)], feat)
    across_bias = bias_ref[...]
    best, numbers = [], []
    for places in ([(back_ref, size), (late_ref, size)], [(late_ref, 0), (late_ref, 2 * size)]):
        best.append(best_of(across_rows, across_bias, places, feat, blocks))
        numbers.append(stack_numbers(places, feat))
    table = slot_table(jnp.concatenate(best, axis=1), jnp.concatenate(numbers, axis=1), blocks)
    out_ref[...] = jnp.maximum(table_ref[...], table)


def vmem():
    return pl.BlockSpec(memory_space=pltpu.VMEM)


def far():
    return pl.BlockSpec(memory_space=pltpu.HBM)


PARAMS = pltpu.CompilerParams(vmem_limit_bytes=48 * 1024 * 1024)


def cost(flops, nbytes):
    return pl.CostEstimate(flops=flops, bytes_accessed=nbytes, transcendentals=0)


def on_device(embeddings, cluster_of, cluster_owner, slot_of, pairs):
    n_owner = lax.axis_size("owner")
    n_group = lax.axis_size("group")
    rows, feat = embeddings.shape
    chunks = feat // LANES
    cap = 3 * rows // (2 * n_owner * n_group)
    lines = UNITS * cap
    pieces = 4
    size = feat + PAY_META
    outgoing = pl.pallas_call(
        lambda *refs: send_kernel(n_owner, n_group, cap, 6, pieces, *refs),
        out_shape=jax.ShapeDtypeStruct((n_owner, lines * chunks + META, LANES), BF16),
        in_specs=[far()] * 4,
        out_specs=vmem(),
        scratch_shapes=[
            pltpu.VMEM((rows, feat), BF16),
            pltpu.VMEM((n_owner * lines * chunks, LANES), F32),
            pltpu.VMEM((1, rows), I32),
            pltpu.VMEM((1, n_owner), I32),
            pltpu.VMEM((1, rows), I32),
            pltpu.SemaphoreType.DMA((pieces + 3,)),
        ],
        compiler_params=PARAMS,
        name="send_rows",
    )(
        *[
            pltpu.with_memory_space_constraint(x, pltpu.HBM)
            for x in (cluster_of.reshape(1, rows), cluster_owner.reshape(1, n_owner), slot_of.reshape(1, rows), embeddings)
        ]
    )
    arrived = lax.all_to_all(outgoing, "owner", split_axis=0, concat_axis=0, tiled=True)
    swap = [(i, i ^ 1) for i in range(n_group)]

    def along_y(x, hops):
        return lax.ppermute(x, "group", [(i, (i + 2 * hops) % n_group) for i in range(n_group)])

    def along_owner(x, hops):
        return lax.ppermute(x, "owner", [(i, (i + hops) % n_owner) for i in range(n_owner)])

    entries = pairs.reshape(-1, 2)
    listed = jnp.pad(entries.T, ((0, 6), (0, LANES - entries.shape[0])), constant_values=-1).astype(F32)
    before, after = along_y(listed, 1), along_y(listed, -1)
    near = jnp.concatenate([before[0:2], listed[0:2], after[0:2], listed[6:8]], axis=0)
    down, up = along_y(near, 3), along_y(near, -3)
    both, first = pl.pallas_call(
        lambda *refs: receive_kernel(n_owner, cap, feat, *refs),
        out_shape=[
            jax.ShapeDtypeStruct((UNITS * size + PAY_META, LANES), BF16),
            jax.ShapeDtypeStruct((size, LANES), BF16),
        ],
        in_specs=[vmem()] * 4,
        out_specs=[vmem()] * 2,
        scratch_shapes=[pltpu.VMEM((n_owner * lines * chunks, LANES), F32)],
        compiler_params=PARAMS,
        name="unit_rows",
    )(arrived, near, up, down)
    twin = lax.ppermute(both, "group", swap)
    following, back = along_y(first, -1), along_y(both, 1)
    high, low = along_owner(both, -1), along_owner(both, 1)
    twin, following, back, high, low = lax.optimization_barrier((twin, following, back, high, low))
    late = lax.ppermute(jnp.concatenate([back[: 2 * size], following], axis=0), "group", swap)
    table, bias = pl.pallas_call(
        lambda *refs: first_score_kernel(n_group, feat, *refs),
        out_shape=[
            jax.ShapeDtypeStruct((n_group, BLOCK), F32),
            jax.ShapeDtypeStruct((4 * BLOCK, n_group), BF16),
        ],
        in_specs=[vmem()] * 6,
        out_specs=[vmem()] * 2,
        compiler_params=PARAMS,
        cost_estimate=cost(3 * 10**9, 4 * 10**6),
        name="score_rows",
    )(both, twin, back, following, low, high)
    table = pl.pallas_call(
        lambda *refs: second_score_kernel(n_group, feat, *refs),
        out_shape=jax.ShapeDtypeStruct((n_group, BLOCK), F32),
        in_specs=[vmem()] * 6,
        out_specs=vmem(),
        compiler_params=PARAMS,
        cost_estimate=cost(5 * 10**8, 2 * 10**6),
        name="score_rest",
    )(table, bias, low, high, back, late)
    shares = lax.all_to_all(table, "group", split_axis=0, concat_axis=0, tiled=True)
    return jnp.max(shares, axis=0, keepdims=True)


def solution(mesh):
    placed = (P("owner", None), P("owner"), P(), P("owner"), P("owner", "group", None, None))
    return jax.shard_map(
        on_device, mesh=mesh, in_specs=placed, out_specs=P("owner", "group"), check_vma=False
    )
```

```python
import jax
import jax.numpy as jnp
from jax import lax
from jax.experimental import pallas as pl
from jax.experimental.pallas import tpu as pltpu
from jax.sharding import PartitionSpec as P

BLOCK = 128
LANES = 128
META = 8
PAY_META = 16
UNITS = 2
BF16 = jnp.bfloat16
F32 = jnp.float32
I32 = jnp.int32


def iota(shape, dim):
    return lax.broadcasted_iota(I32, shape, dim)


def ones_where(mask):
    return jnp.where(mask, 1.0, 0.0).astype(BF16)


def mm(a, b):
    return jnp.dot(a, b, preferred_element_type=F32)


def mm_nt(a, b):
    return lax.dot_general(a, b, (((1,), (1,)), ((), ())), preferred_element_type=F32)


def mm_tn(a, b):
    return lax.dot_general(a, b, (((0,), (0,)), ((), ())), preferred_element_type=F32)


def send_kernel(n_owner, n_group, cap, shift, pieces, cluster_hbm, owner_hbm, slot_hbm, emb_ref, out_ref, emb, wide, cluster_ref, owner_ref, slot_ref, sems):
    rows, feat = emb.shape
    chunks = feat // LANES
    step = rows // pieces
    small = [
        pltpu.make_async_copy(source, goal, sems.at[pieces + i])
        for i, (source, goal) in enumerate(
            ((cluster_hbm, cluster_ref), (owner_hbm, owner_ref), (slot_hbm, slot_ref))
        )
    ]
    copies = [
        pltpu.make_async_copy(emb_ref.at[pl.ds(i * step, step)], emb.at[pl.ds(i * step, step)], sems.at[i])
        for i in range(pieces)
    ]
    for copy in small + copies:
        copy.start()
    for copy in small:
        copy.wait()
    me = lax.axis_index("group")
    picked = ones_where(iota((n_owner, rows), 0) == cluster_ref[...])
    table = ones_where(iota((n_owner, n_owner), 0) == owner_ref[...])
    to = mm(table, picked).astype(BF16)
    parts = rows // LANES
    stacked = jnp.concatenate([to[:, i * LANES : (i + 1) * LANES] for i in range(parts)], axis=0)
    before = mm(stacked, ones_where(iota((LANES, LANES), 0) < iota((LANES, LANES), 1)))
    totals = mm(stacked, jnp.ones((LANES, LANES), BF16))
    running = jnp.zeros((n_owner, LANES), F32)
    lane_owner = iota((n_owner, LANES), 0).astype(F32)
    place, target = [], []
    for i in range(parts):
        here = stacked[i * n_owner : (i + 1) * n_owner].astype(F32)
        spot = before[i * n_owner : (i + 1) * n_owner] + running
        place.append(jnp.sum(here * spot, axis=0, keepdims=True))
        target.append(jnp.sum(here * lane_owner, axis=0, keepdims=True))
        running = running + totals[i * n_owner : (i + 1) * n_owner]
    place = jnp.concatenate(place, axis=1).astype(I32)
    target = jnp.concatenate(target, axis=1).astype(I32)
    share = place & (n_group - 1)
    entry = place // n_group
    entry = jnp.where(share == me, entry, jnp.where(share == ((me + shift) & (n_group - 1)), entry + cap, -1))
    mine = entry >= 0
    lines = UNITS * cap
    goal = jnp.where(mine, target * lines + entry, -1)
    slot = slot_ref[...]
    high = (slot // BLOCK + 1).astype(F32)
    low = (slot & (BLOCK - 1)).astype(F32)
    at_entry = iota((LANES, rows), 0) == entry
    meta_high = mm_nt(to, jnp.where(at_entry, high, 0.0).astype(BF16)).astype(BF16)
    meta_low = mm_nt(to, jnp.where(at_entry, low, 0.0).astype(BF16)).astype(BF16)
    line = iota((n_owner * META, n_owner), 0)
    peer = iota((n_owner * META, n_owner), 1)
    meta = mm(ones_where(line == peer * META), meta_high) + mm(ones_where(line == peer * META + 1), meta_low)
    out_ref[:, lines * chunks :, :] = meta.reshape(n_owner, META, LANES).astype(BF16)
    select = ones_where(iota((n_owner * lines, rows), 0) == goal)
    total = None
    for i, copy in enumerate(copies):
        copy.wait()
        part = mm(select[:, i * step : (i + 1) * step], emb[pl.ds(i * step, step), :])
        total = part if total is None else total + part
    for k in range(chunks):
        wide[pl.ds(k, n_owner * lines, chunks), :] = total[:, k * LANES : (k + 1) * LANES]
    out_ref[:, : lines * chunks, :] = wide[...].reshape(n_owner, lines * chunks, LANES).astype(BF16)


def receive_kernel(n_owner, cap, feat, in_ref, near_ref, up_ref, down_ref, both_ref, first_ref, wide):
    chunks = feat // LANES
    per_peer = UNITS * cap
    lines = n_owner * per_peer
    size = feat + PAY_META
    wide[...] = in_ref[:, : per_peer * chunks, :].astype(F32).reshape(lines * chunks, LANES)
    meta = in_ref[:, per_peer * chunks :, :].astype(F32).reshape(n_owner * META, LANES).astype(BF16)
    line = iota((lines, n_owner * META), 0)
    source = iota((lines, n_owner * META), 1)
    at_lane = iota((lines, LANES), 1) == lax.rem(iota((lines, LANES), 0), per_peer)
    high = mm(ones_where(source == line // per_peer * META), meta)
    low = mm(ones_where(source == line // per_peer * META + 1), meta)
    ones = jnp.ones((LANES, LANES), BF16)
    high = mm(jnp.where(at_lane, high, 0.0).astype(BF16), ones)
    low = mm(jnp.where(at_lane, low, 0.0).astype(BF16), ones)
    valid = ones_where(high > 0.5)
    later, sooner = iota((lines, lines), 0), iota((lines, lines), 1)
    same = lax.rem(later, per_peer) // cap == lax.rem(sooner, per_peer) // cap
    place = mm(ones_where(jnp.logical_and(sooner < later, same)), valid)
    unit = lax.rem(iota((lines, BLOCK), 0), per_peer) // cap
    here = jnp.logical_and(place == iota((lines, BLOCK), 1).astype(F32), high > 0.5)
    puts = [jnp.logical_and(here, unit == n) for n in range(UNITS)]
    put_one = ones_where(jnp.concatenate(puts, axis=1))
    parts = []
    square = None
    for k in range(chunks):
        part = mm_tn(put_one, wide[pl.ds(k, lines, chunks), :].astype(BF16))
        parts.append(part)
        here = part * part
        square = here if square is None else square + here
    scale = lax.rsqrt(jnp.sum(square, axis=1, keepdims=True) + 1e-06)
    for k in range(chunks):
        piece = (parts[k] * scale).astype(BF16)
        for n in range(UNITS):
            both_ref[pl.ds(n * size + k * BLOCK, BLOCK), :] = piece[n * BLOCK : (n + 1) * BLOCK]
        first_ref[pl.ds(k * BLOCK, BLOCK), :] = piece[:BLOCK]
    row = iota((PAY_META, LANES), 0)
    for n in range(UNITS):
        blocks = jnp.sum(jnp.where(puts[n], high, 0.0), axis=0, keepdims=True) - 1.0
        inner = jnp.sum(jnp.where(puts[n], low, 0.0), axis=0, keepdims=True)
        numbers = jnp.where(row == 0, blocks, jnp.where(row == 1, inner, 0.0)).astype(BF16)
        both_ref[pl.ds(n * size + feat, PAY_META), :] = numbers
        if n == 0:
            first_ref[pl.ds(feat, PAY_META), :] = numbers
    lists = jnp.concatenate([near_ref[0:6, :], up_ref[0:6, :], down_ref[2:6, :]], axis=0)
    both_ref[pl.ds(UNITS * size, PAY_META), :] = lists.astype(BF16)


def rows_of(ref, start, feat):
    return jnp.concatenate([ref[pl.ds(start + k * BLOCK, BLOCK), :] for k in range(feat // LANES)], axis=1)


def numbers_of(ref, start, feat):
    return ref[pl.ds(start + feat, PAY_META), :].astype(F32)[0:2, :].astype(I32)


def stack_rows(places, feat):
    return jnp.concatenate([rows_of(ref, start, feat) for ref, start in places], axis=0)


def stack_numbers(places, feat):
    return jnp.concatenate([numbers_of(ref, start, feat) for ref, start in places], axis=1)


def best_of(left, bias, places, feat, blocks, same=None):
    right = stack_rows(places, feat)
    width = right.shape[0]
    here = ones_where(iota((blocks, width), 0) == stack_numbers(places, feat)[0:1, :])
    scores = mm_nt(left, right) + mm(bias, here)
    if same is not None:
        scores = jnp.where(same, -2.0, scores)
    return jnp.max(scores, axis=0, keepdims=True)


def bias_of(penalty, marks):
    picked = ones_where(iota((penalty.shape[0], marks.shape[1]), 0) == marks)
    return mm_tn(picked, penalty).astype(BF16)


def slot_table(best, numbers, blocks):
    total = best.shape[1]
    best = jnp.maximum(best, -2.0)
    spread = iota((blocks, total), 0) == numbers[0:1, :]
    inner = ones_where(iota((BLOCK, total), 0) == numbers[1:2, :])
    filled = mm_nt(ones_where(spread), inner)
    result = jnp.zeros((blocks, BLOCK), F32)
    rest = best
    for _ in range(3):
        piece = rest.astype(BF16).astype(F32)
        rest = rest - piece
        result += mm_nt(jnp.where(spread, piece, 0.0).astype(BF16), inner)
    return jnp.where(filled > 0.5, result, -2.0)


def first_score_kernel(blocks, feat, own_ref, twin_ref, back_ref, next_ref, low_ref, high_ref, out_ref, bias_ref):
    size = feat + PAY_META
    lists = [r[pl.ds(UNITS * size, PAY_META), :].astype(F32) for r in (own_ref, twin_ref)]
    count = PAY_META // 2

    def list_row(i):
        return jnp.concatenate([n[2 * b + i : 2 * b + i + 1, :] for n in lists for b in range(count)], axis=1).astype(I32)

    first, second = list_row(0), list_row(1)
    total = 2 * count * LANES
    first_rows = iota((blocks, total), 0)
    wide_rows = iota((3 * blocks, total), 0)
    paired = mm_nt(ones_where(wide_rows == second), ones_where(first_rows == first))
    paired += mm_nt(ones_where(wide_rows == first + blocks), ones_where(first_rows == second - blocks))
    penalty = jnp.where(paired > 0.5, 0.0, -4.0).astype(BF16)
    across = [(low_ref, 0), (low_ref, size), (high_ref, 0), (high_ref, size)]
    marks = stack_numbers(across, feat)[0:1, :]
    marks += jnp.where(iota(marks.shape, 1) < 2 * BLOCK, 0, 2 * blocks)
    across_bias = bias_of(penalty, marks)
    bias_ref[...] = across_bias
    across_rows = stack_rows(across, feat)
    inside = [(back_ref, 0), (next_ref, 0), (own_ref, 0), (twin_ref, 0), (own_ref, size), (twin_ref, size)]
    inside_bias = bias_of(penalty, stack_numbers(inside, feat)[0:1, :] + blocks)
    inside_rows = stack_rows(inside, feat)
    row, lane = iota((6 * BLOCK, 2 * BLOCK), 0), iota((6 * BLOCK, 2 * BLOCK), 1)
    same = row == lane + jnp.where(lane < BLOCK, 2 * BLOCK, 3 * BLOCK)
    groups = [
        ([(own_ref, 0), (own_ref, size)], 0, 6, same),
        ([(twin_ref, 0), (twin_ref, size)], 0, 3, None),
        ([(back_ref, 0), (next_ref, 0)], 2, 6, None),
    ]
    best, numbers = [], []
    for places, low, high, equal in groups:
        part = slice(low * BLOCK, high * BLOCK)
        one = best_of(across_rows, across_bias, places, feat, blocks)
        two = best_of(inside_rows[part], inside_bias[part], places, feat, blocks, equal)
        best.append(jnp.maximum(one, two))
        numbers.append(stack_numbers(places, feat))
    out_ref[...] = slot_table(jnp.concatenate(best, axis=1), jnp.concatenate(numbers, axis=1), blocks)


def second_score_kernel(blocks, feat, table_ref, bias_ref, low_ref, high_ref, back_ref, late_ref, out_ref):
    size = feat + PAY_META
    across_rows = stack_rows([(low_ref, 0), (low_ref, size), (high_ref, 0), (high_ref, size)], feat)
    across_bias = bias_ref[...]
    best, numbers = [], []
    for places in ([(back_ref, size), (late_ref, size)], [(late_ref, 0), (late_ref, 2 * size)]):
        best.append(best_of(across_rows, across_bias, places, feat, blocks))
        numbers.append(stack_numbers(places, feat))
    table = slot_table(jnp.concatenate(best, axis=1), jnp.concatenate(numbers, axis=1), blocks)
    table = jnp.maximum(table_ref[...], table)
    for b in range(blocks):
        out_ref[b] = jnp.broadcast_to(table[b : b + 1, :], (8, BLOCK))


def vmem():
    return pl.BlockSpec(memory_space=pltpu.VMEM)


def far():
    return pl.BlockSpec(memory_space=pltpu.HBM)


PARAMS = pltpu.CompilerParams(vmem_limit_bytes=48 * 1024 * 1024)


def cost(flops, nbytes):
    return pl.CostEstimate(flops=flops, bytes_accessed=nbytes, transcendentals=0)


def on_device(embeddings, cluster_of, cluster_owner, slot_of, pairs):
    n_owner = lax.axis_size("owner")
    n_group = lax.axis_size("group")
    rows, feat = embeddings.shape
    chunks = feat // LANES
    cap = 3 * rows // (2 * n_owner * n_group)
    lines = UNITS * cap
    pieces = 4
    size = feat + PAY_META
    outgoing = pl.pallas_call(
        lambda *refs: send_kernel(n_owner, n_group, cap, 6, pieces, *refs),
        out_shape=jax.ShapeDtypeStruct((n_owner, lines * chunks + META, LANES), BF16),
        in_specs=[far()] * 4,
        out_specs=vmem(),
        scratch_shapes=[
            pltpu.VMEM((rows, feat), BF16),
            pltpu.VMEM((n_owner * lines * chunks, LANES), F32),
            pltpu.VMEM((1, rows), I32),
            pltpu.VMEM((1, n_owner), I32),
            pltpu.VMEM((1, rows), I32),
            pltpu.SemaphoreType.DMA((pieces + 3,)),
        ],
        compiler_params=PARAMS,
        name="send_rows",
    )(
        *[
            pltpu.with_memory_space_constraint(x, pltpu.HBM)
            for x in (cluster_of.reshape(1, rows), cluster_owner.reshape(1, n_owner), slot_of.reshape(1, rows), embeddings)
        ]
    )
    arrived = lax.all_to_all(outgoing, "owner", split_axis=0, concat_axis=0, tiled=True)
    swap = [(i, i ^ 1) for i in range(n_group)]

    def along_y(x, hops):
        return lax.ppermute(x, "group", [(i, (i + 2 * hops) % n_group) for i in range(n_group)])

    def along_owner(x, hops):
        return lax.ppermute(x, "owner", [(i, (i + hops) % n_owner) for i in range(n_owner)])

    entries = pairs.reshape(-1, 2)
    listed = jnp.pad(entries.T, ((0, 6), (0, LANES - entries.shape[0])), constant_values=-1).astype(F32)
    before, after = along_y(listed, 1), along_y(listed, -1)
    near = jnp.concatenate([before[0:2], listed[0:2], after[0:2], listed[6:8]], axis=0)
    down, up = along_y(near, 3), along_y(near, -3)
    both, first = pl.pallas_call(
        lambda *refs: receive_kernel(n_owner, cap, feat, *refs),
        out_shape=[
            jax.ShapeDtypeStruct((UNITS * size + PAY_META, LANES), BF16),
            jax.ShapeDtypeStruct((size, LANES), BF16),
        ],
        in_specs=[vmem()] * 4,
        out_specs=[vmem()] * 2,
        scratch_shapes=[pltpu.VMEM((n_owner * lines * chunks, LANES), F32)],
        compiler_params=PARAMS,
        name="unit_rows",
    )(arrived, near, up, down)
    twin = lax.ppermute(both, "group", swap)
    following, back = along_y(first, -1), along_y(both, 1)
    high, low = along_owner(both, -1), along_owner(both, 1)
    following, back, high, low = lax.optimization_barrier((following, back, high, low))
    late = lax.ppermute(jnp.concatenate([back[: 2 * size], following], axis=0), "group", swap)
    table, bias = pl.pallas_call(
        lambda *refs: first_score_kernel(n_group, feat, *refs),
        out_shape=[
            jax.ShapeDtypeStruct((n_group, BLOCK), F32),
            jax.ShapeDtypeStruct((4 * BLOCK, n_group), BF16),
        ],
        in_specs=[vmem()] * 6,
        out_specs=[vmem()] * 2,
        compiler_params=PARAMS,
        cost_estimate=cost(3 * 10**9, 4 * 10**6),
        name="score_rows",
    )(both, twin, back, following, low, high)
    table = pl.pallas_call(
        lambda *refs: second_score_kernel(n_group, feat, *refs),
        out_shape=jax.ShapeDtypeStruct((n_group, 8, BLOCK), F32),
        in_specs=[vmem()] * 6,
        out_specs=vmem(),
        compiler_params=PARAMS,
        cost_estimate=cost(5 * 10**8, 2 * 10**6),
        name="score_rest",
    )(table, bias, low, high, back, late)
    shares = lax.all_to_all(table, "group", split_axis=0, concat_axis=0, tiled=True)
    return jnp.max(shares[:, :1], axis=0)


def solution(mesh):
    placed = (P("owner", None), P("owner"), P(), P("owner"), P("owner", "group", None, None))
    return jax.shard_map(
        on_device, mesh=mesh, in_specs=placed, out_specs=P("owner", "group"), check_vma=False
    )
```

```python
import jax
import jax.numpy as jnp
from jax import lax
from jax.experimental import pallas as pl
from jax.experimental.pallas import tpu as pltpu
from jax.sharding import PartitionSpec as P

BLOCK = 128
LANES = 128
META = 8
PAY_META = 16
UNITS = 2
BF16 = jnp.bfloat16
F32 = jnp.float32
I32 = jnp.int32


def iota(shape, dim):
    return lax.broadcasted_iota(I32, shape, dim)


def ones_where(mask):
    return jnp.where(mask, 1.0, 0.0).astype(BF16)


def mm(a, b):
    return jnp.dot(a, b, preferred_element_type=F32)


def mm_nt(a, b):
    return lax.dot_general(a, b, (((1,), (1,)), ((), ())), preferred_element_type=F32)


def mm_tn(a, b):
    return lax.dot_general(a, b, (((0,), (0,)), ((), ())), preferred_element_type=F32)


def send_kernel(n_owner, n_group, cap, shift, pieces, cluster_hbm, owner_hbm, slot_hbm, emb_ref, out_ref, emb, wide, cluster_ref, owner_ref, slot_ref, sems):
    rows, feat = emb.shape
    chunks = feat // LANES
    step = rows // pieces
    small = [
        pltpu.make_async_copy(source, goal, sems.at[pieces + i])
        for i, (source, goal) in enumerate(
            ((cluster_hbm, cluster_ref), (owner_hbm, owner_ref), (slot_hbm, slot_ref))
        )
    ]
    copies = [
        pltpu.make_async_copy(emb_ref.at[pl.ds(i * step, step)], emb.at[pl.ds(i * step, step)], sems.at[i])
        for i in range(pieces)
    ]
    for copy in small + copies:
        copy.start()
    for copy in small:
        copy.wait()
    me = lax.axis_index("group")
    picked = ones_where(iota((n_owner, rows), 0) == cluster_ref[...])
    table = ones_where(iota((n_owner, n_owner), 0) == owner_ref[...])
    to = mm(table, picked).astype(BF16)
    parts = rows // LANES
    stacked = jnp.concatenate([to[:, i * LANES : (i + 1) * LANES] for i in range(parts)], axis=0)
    before = mm(stacked, ones_where(iota((LANES, LANES), 0) < iota((LANES, LANES), 1)))
    totals = mm(stacked, jnp.ones((LANES, LANES), BF16))
    running = jnp.zeros((n_owner, LANES), F32)
    lane_owner = iota((n_owner, LANES), 0).astype(F32)
    place, target = [], []
    for i in range(parts):
        here = stacked[i * n_owner : (i + 1) * n_owner].astype(F32)
        spot = before[i * n_owner : (i + 1) * n_owner] + running
        place.append(jnp.sum(here * spot, axis=0, keepdims=True))
        target.append(jnp.sum(here * lane_owner, axis=0, keepdims=True))
        running = running + totals[i * n_owner : (i + 1) * n_owner]
    place = jnp.concatenate(place, axis=1).astype(I32)
    target = jnp.concatenate(target, axis=1).astype(I32)
    share = place & (n_group - 1)
    entry = place // n_group
    entry = jnp.where(share == me, entry, jnp.where(share == ((me + shift) & (n_group - 1)), entry + cap, -1))
    mine = entry >= 0
    lines = UNITS * cap
    goal = jnp.where(mine, target * lines + entry, -1)
    slot = slot_ref[...]
    high = (slot // BLOCK + 1).astype(F32)
    low = (slot & (BLOCK - 1)).astype(F32)
    width = 16
    row = iota((2 * width, rows), 0)
    values = jnp.where((row & (width - 1)) == entry, jnp.where(row < width, high, low), 0.0).astype(BF16)
    meta = mm_nt(to, values).astype(BF16)
    line = iota((n_owner * META, n_owner), 0)
    peer = iota((n_owner * META, n_owner), 1)
    meta = mm(ones_where(line // META == peer), meta)
    line = iota((n_owner * META, 2 * width), 0) & (META - 1)
    meta = jnp.where(iota((n_owner * META, 2 * width), 1) // width == line, meta, 0.0).astype(BF16)
    column = iota((2 * width, LANES), 0) & (width - 1)
    meta = mm(meta, ones_where(column == iota((2 * width, LANES), 1)))
    out_ref[:, lines * chunks :, :] = meta.reshape(n_owner, META, LANES).astype(BF16)
    select = ones_where(iota((n_owner * lines, rows), 0) == goal)
    total = None
    for i, copy in enumerate(copies[:-1]):
        copy.wait()
        part = mm(select[:, i * step : (i + 1) * step], emb[pl.ds(i * step, step), :])
        total = part if total is None else total + part
    copies[-1].wait()
    last = rows - step
    for k in range(0, chunks, 2):
        part = total[:, k * LANES : (k + 2) * LANES]
        part += mm(select[:, last:], emb[pl.ds(last, step), pl.ds(k * LANES, 2 * LANES)])
        for h in range(2):
            wide[pl.ds(k + h, n_owner * lines, chunks), :] = part[:, h * LANES : (h + 1) * LANES]
    out_ref[:, : lines * chunks, :] = wide[...].reshape(n_owner, lines * chunks, LANES).astype(BF16)


def receive_kernel(n_owner, cap, feat, in_ref, here_ref, there_ref, both_ref, first_ref, wide):
    chunks = feat // LANES
    per_peer = UNITS * cap
    lines = n_owner * per_peer
    size = feat + PAY_META
    wide[...] = in_ref[:, : per_peer * chunks, :].astype(F32).reshape(lines * chunks, LANES)
    meta = in_ref[:, per_peer * chunks :, :].astype(F32).reshape(n_owner * META, LANES).astype(BF16)
    line = iota((lines, n_owner * META), 0)
    source = iota((lines, n_owner * META), 1)
    at_lane = iota((lines, LANES), 1) == lax.rem(iota((lines, LANES), 0), per_peer)
    high = mm(ones_where(source == line // per_peer * META), meta)
    low = mm(ones_where(source == line // per_peer * META + 1), meta)
    ones = jnp.ones((LANES, LANES), BF16)
    high = mm(jnp.where(at_lane, high, 0.0).astype(BF16), ones)
    low = mm(jnp.where(at_lane, low, 0.0).astype(BF16), ones)
    valid = ones_where(high > 0.5)
    later, sooner = iota((lines, lines), 0), iota((lines, lines), 1)
    same = lax.rem(later, per_peer) // cap == lax.rem(sooner, per_peer) // cap
    place = mm(ones_where(jnp.logical_and(sooner < later, same)), valid)
    unit = lax.rem(iota((lines, BLOCK), 0), per_peer) // cap
    here = jnp.logical_and(place == iota((lines, BLOCK), 1).astype(F32), high > 0.5)
    puts = [jnp.logical_and(here, unit == n) for n in range(UNITS)]
    put_one = ones_where(jnp.concatenate(puts, axis=1))
    parts = []
    square = None
    for k in range(chunks):
        part = mm_tn(put_one, wide[pl.ds(k, lines, chunks), :].astype(BF16))
        parts.append(part)
        here = part * part
        square = here if square is None else square + here
    scale = lax.rsqrt(jnp.sum(square, axis=1, keepdims=True) + 1e-06)
    for k in range(chunks):
        piece = (parts[k] * scale).astype(BF16)
        for n in range(UNITS):
            both_ref[pl.ds(n * size + k * BLOCK, BLOCK), :] = piece[n * BLOCK : (n + 1) * BLOCK]
        first_ref[pl.ds(k * BLOCK, BLOCK), :] = piece[:BLOCK]
    row = iota((PAY_META, LANES), 0)
    for n in range(UNITS):
        blocks = jnp.sum(jnp.where(puts[n], high, 0.0), axis=0, keepdims=True) - 1.0
        inner = jnp.sum(jnp.where(puts[n], low, 0.0), axis=0, keepdims=True)
        numbers = jnp.where(row == 0, blocks, jnp.where(row == 1, inner, 0.0)).astype(BF16)
        both_ref[pl.ds(n * size + feat, PAY_META), :] = numbers
        if n == 0:
            first_ref[pl.ds(feat, PAY_META), :] = numbers
    lists = jnp.concatenate([here_ref[...], there_ref[...]], axis=0)
    both_ref[pl.ds(UNITS * size, PAY_META), :] = lists.astype(BF16)


def rows_of(ref, start, feat):
    return jnp.concatenate([ref[pl.ds(start + k * BLOCK, BLOCK), :] for k in range(feat // LANES)], axis=1)


def numbers_of(ref, start, feat):
    return ref[pl.ds(start + feat, PAY_META), :].astype(F32)[0:2, :].astype(I32)


def stack_rows(places, feat):
    return jnp.concatenate([rows_of(ref, start, feat) for ref, start in places], axis=0)


def stack_numbers(places, feat):
    return jnp.concatenate([numbers_of(ref, start, feat) for ref, start in places], axis=1)


def best_of(left, bias, places, feat, blocks, same=None):
    right = stack_rows(places, feat)
    width = right.shape[0]
    here = ones_where(iota((blocks, width), 0) == stack_numbers(places, feat)[0:1, :])
    scores = mm_nt(left, right) + mm(bias, here)
    if same is not None:
        scores = jnp.where(same, -2.0, scores)
    return jnp.max(scores, axis=0, keepdims=True)


def bias_of(penalty, marks):
    picked = ones_where(iota((penalty.shape[0], marks.shape[1]), 0) == marks)
    return mm_tn(picked, penalty).astype(BF16)


def slot_table(best, numbers, blocks):
    total = best.shape[1]
    best = jnp.maximum(best, -2.0)
    spread = iota((blocks, total), 0) == numbers[0:1, :]
    inner = ones_where(iota((BLOCK, total), 0) == numbers[1:2, :])
    filled = mm_nt(ones_where(spread), inner)
    result = jnp.zeros((blocks, BLOCK), F32)
    rest = best
    for _ in range(3):
        piece = rest.astype(BF16).astype(F32)
        rest = rest - piece
        result += mm_nt(jnp.where(spread, piece, 0.0).astype(BF16), inner)
    return jnp.where(filled > 0.5, result, -2.0)


def first_score_kernel(blocks, feat, own_ref, twin_ref, back_ref, next_ref, left_ref, right_ref, out_ref, bias_ref):
    size = feat + PAY_META
    lists = [r[pl.ds(UNITS * size, PAY_META), :].astype(F32) for r in (own_ref, twin_ref)]
    count = PAY_META // 2

    def list_row(i):
        return jnp.concatenate([n[2 * b + i : 2 * b + i + 1, :] for n in lists for b in range(count)], axis=1).astype(I32)

    first, second = list_row(0), list_row(1)
    total = 2 * count * LANES
    first_rows = iota((blocks, total), 0)
    wide_rows = iota((3 * blocks, total), 0)
    paired = mm_nt(ones_where(wide_rows == second), ones_where(first_rows == first))
    paired += mm_nt(ones_where(wide_rows == first + blocks), ones_where(first_rows == second - blocks))
    penalty = jnp.where(paired > 0.5, 0.0, -4.0).astype(BF16)
    across = [(left_ref, 0), (right_ref, 0), (left_ref, size), (right_ref, size)]
    marks = stack_numbers(across, feat)[0:1, :]
    odd = lax.axis_index("owner") & 1
    marks += 2 * blocks * jnp.where((iota(marks.shape, 1) & BLOCK) == 0, 1 - odd, odd)
    across_bias = bias_of(penalty, marks)
    bias_ref[...] = across_bias
    across_rows = stack_rows(across, feat)
    inside = [(next_ref, 0), (back_ref, 0), (own_ref, 0), (twin_ref, 0), (own_ref, size), (twin_ref, size)]
    inside_bias = bias_of(penalty, stack_numbers(inside, feat)[0:1, :] + blocks)
    inside_rows = stack_rows(inside, feat)
    row, lane = iota((5 * BLOCK, 2 * BLOCK), 0), iota((5 * BLOCK, 2 * BLOCK), 1)
    groups = [
        ([(own_ref, 0), (twin_ref, 0)], 4, 1, 6, row == lane + BLOCK),
        ([(own_ref, size), (twin_ref, size)], 2, 0, 3, None),
        ([(back_ref, 0), (next_ref, 0)], 4, 2, 6, None),
    ]
    best, numbers = [], []
    for places, count, low, high, equal in groups:
        part = slice(low * BLOCK, high * BLOCK)
        outer = slice(0, count * BLOCK)
        one = best_of(across_rows[outer], across_bias[outer], places, feat, blocks)
        two = best_of(inside_rows[part], inside_bias[part], places, feat, blocks, equal)
        best.append(jnp.maximum(one, two))
        numbers.append(stack_numbers(places, feat))
    out_ref[...] = slot_table(jnp.concatenate(best, axis=1), jnp.concatenate(numbers, axis=1), blocks)


def second_score_kernel(blocks, feat, table_ref, bias_ref, left_ref, right_ref, back_ref, late_ref, out_ref):
    size = feat + PAY_META
    across_rows = stack_rows([(left_ref, 0), (right_ref, 0), (left_ref, size), (right_ref, size)], feat)
    across_bias = bias_ref[...]
    best, numbers = [], []
    for places, count in (([(back_ref, size), (late_ref, size)], 2), ([(late_ref, 0), (late_ref, 2 * size)], 4)):
        outer = slice(0, count * BLOCK)
        best.append(best_of(across_rows[outer], across_bias[outer], places, feat, blocks))
        numbers.append(stack_numbers(places, feat))
    table = slot_table(jnp.concatenate(best, axis=1), jnp.concatenate(numbers, axis=1), blocks)
    table = jnp.maximum(table_ref[...], table)
    for b in range(blocks):
        out_ref[b] = jnp.broadcast_to(table[b : b + 1, :], (8, BLOCK))


def vmem():
    return pl.BlockSpec(memory_space=pltpu.VMEM)


def far():
    return pl.BlockSpec(memory_space=pltpu.HBM)


PARAMS = pltpu.CompilerParams(vmem_limit_bytes=48 * 1024 * 1024)


def cost(flops, nbytes):
    return pl.CostEstimate(flops=flops, bytes_accessed=nbytes, transcendentals=0)


def on_device(embeddings, cluster_of, cluster_owner, slot_of, pairs):
    n_owner = lax.axis_size("owner")
    n_group = lax.axis_size("group")
    rows, feat = embeddings.shape
    chunks = feat // LANES
    cap = 3 * rows // (2 * n_owner * n_group)
    lines = UNITS * cap
    pieces = 4
    size = feat + PAY_META
    outgoing = pl.pallas_call(
        lambda *refs: send_kernel(n_owner, n_group, cap, 6, pieces, *refs),
        out_shape=jax.ShapeDtypeStruct((n_owner, lines * chunks + META, LANES), BF16),
        in_specs=[far()] * 4,
        out_specs=vmem(),
        scratch_shapes=[
            pltpu.VMEM((rows, feat), BF16),
            pltpu.VMEM((n_owner * lines * chunks, LANES), F32),
            pltpu.VMEM((1, rows), I32),
            pltpu.VMEM((1, n_owner), I32),
            pltpu.VMEM((1, rows), I32),
            pltpu.SemaphoreType.DMA((pieces + 3,)),
        ],
        compiler_params=PARAMS,
        name="send_rows",
    )(
        *[
            pltpu.with_memory_space_constraint(x, pltpu.HBM)
            for x in (cluster_of.reshape(1, rows), cluster_owner.reshape(1, n_owner), slot_of.reshape(1, rows), embeddings)
        ]
    )
    arrived = lax.all_to_all(outgoing, "owner", split_axis=0, concat_axis=0, tiled=True)
    swap = [(i, i ^ 1) for i in range(n_group)]

    def along_y(x, partner):
        return lax.ppermute(x, "group", [(i, 2 * (partner(i // 2) % (n_group // 2)) + i % 2) for i in range(n_group)])

    def along_owner(x, partner):
        return lax.ppermute(x, "owner", [(i, partner(i) % n_owner) for i in range(n_owner)])

    entries = pairs.reshape(-1, 2)
    here = jnp.pad(entries.T, ((0, 0), (0, LANES - entries.shape[0])), constant_values=-1).astype(F32)
    blank = jnp.full((6, LANES), -1.0, F32)
    there = along_y(jnp.concatenate([here, blank], axis=0), lambda y: y ^ 1)
    here = jnp.concatenate([here, there[:2]], axis=0)
    there = along_y(jnp.concatenate([here, blank[:4]], axis=0), lambda y: y ^ 2)
    here = jnp.concatenate([here, there[:4]], axis=0)
    there = along_y(here, lambda y: y ^ 4)
    both, first = pl.pallas_call(
        lambda *refs: receive_kernel(n_owner, cap, feat, *refs),
        out_shape=[
            jax.ShapeDtypeStruct((UNITS * size + PAY_META, LANES), BF16),
            jax.ShapeDtypeStruct((size, LANES), BF16),
        ],
        in_specs=[vmem()] * 3,
        out_specs=[vmem()] * 2,
        scratch_shapes=[pltpu.VMEM((n_owner * lines * chunks, LANES), F32)],
        compiler_params=PARAMS,
        name="unit_rows",
    )(arrived, here, there)
    twin = lax.ppermute(both, "group", swap)
    following, back = along_y(first, lambda y: y - 1), along_y(both, lambda y: y + 1)
    left, right = along_owner(both, lambda o: o ^ 1), along_owner(both, lambda o: o + 2 * (o & 1) - 1)
    following, right, back, left = lax.optimization_barrier((following, right, back, left))
    late = lax.ppermute(jnp.concatenate([back[: 2 * size], following], axis=0), "group", swap)
    table, bias = pl.pallas_call(
        lambda *refs: first_score_kernel(n_group, feat, *refs),
        out_shape=[
            jax.ShapeDtypeStruct((n_group, BLOCK), F32),
            jax.ShapeDtypeStruct((4 * BLOCK, n_group), BF16),
        ],
        in_specs=[vmem()] * 6,
        out_specs=[vmem()] * 2,
        compiler_params=PARAMS,
        cost_estimate=cost(3 * 10**9, 4 * 10**6),
        name="score_rows",
    )(both, twin, back, following, left, right)
    table = pl.pallas_call(
        lambda *refs: second_score_kernel(n_group, feat, *refs),
        out_shape=jax.ShapeDtypeStruct((n_group, 8, BLOCK), F32),
        in_specs=[vmem()] * 6,
        out_specs=vmem(),
        compiler_params=PARAMS,
        cost_estimate=cost(5 * 10**8, 2 * 10**6),
        name="score_rest",
    )(table, bias, left, right, back, late)
    shares = lax.all_to_all(table, "group", split_axis=0, concat_axis=0, tiled=True)
    return jnp.max(shares[:, :1], axis=0)


def solution(mesh):
    placed = (P("owner", None), P("owner"), P(), P("owner"), P("owner", "group", None, None))
    return jax.shard_map(
        on_device, mesh=mesh, in_specs=placed, out_specs=P("owner", "group"), check_vma=False
    )
```

```python
import jax
import jax.numpy as jnp
from jax import lax
from jax.experimental import pallas as pl
from jax.experimental.pallas import tpu as pltpu
from jax.sharding import PartitionSpec as P

BLOCK = 128
LANES = 128
META = 8
PAY_META = 16
UNITS = 2
BF16 = jnp.bfloat16
F32 = jnp.float32
I32 = jnp.int32


def iota(shape, dim):
    return lax.broadcasted_iota(I32, shape, dim)


def ones_where(mask):
    return jnp.where(mask, 1.0, 0.0).astype(BF16)


def mm(a, b):
    return jnp.dot(a, b, preferred_element_type=F32)


def mm_nt(a, b):
    return lax.dot_general(a, b, (((1,), (1,)), ((), ())), preferred_element_type=F32)


def mm_tn(a, b):
    return lax.dot_general(a, b, (((0,), (0,)), ((), ())), preferred_element_type=F32)


def send_kernel(n_owner, n_group, cap, shift, pieces, cluster_hbm, owner_hbm, slot_hbm, emb_ref, out_ref, emb, wide, cluster_ref, owner_ref, slot_ref, sems):
    rows, feat = emb.shape
    chunks = feat // LANES
    step = rows // pieces
    small = [
        pltpu.make_async_copy(source, goal, sems.at[pieces + i])
        for i, (source, goal) in enumerate(
            ((cluster_hbm, cluster_ref), (owner_hbm, owner_ref), (slot_hbm, slot_ref))
        )
    ]
    copies = [
        pltpu.make_async_copy(emb_ref.at[pl.ds(i * step, step)], emb.at[pl.ds(i * step, step)], sems.at[i])
        for i in range(pieces)
    ]
    for copy in small + copies:
        copy.start()
    for copy in small:
        copy.wait()
    me = lax.axis_index("group")
    picked = ones_where(iota((n_owner, rows), 0) == cluster_ref[...])
    table = ones_where(iota((n_owner, n_owner), 0) == owner_ref[...])
    to = mm(table, picked).astype(BF16)
    parts = rows // LANES
    stacked = jnp.concatenate([to[:, i * LANES : (i + 1) * LANES] for i in range(parts)], axis=0)
    before = mm(stacked, ones_where(iota((LANES, LANES), 0) < iota((LANES, LANES), 1)))
    totals = mm(stacked, jnp.ones((LANES, LANES), BF16))
    running = jnp.zeros((n_owner, LANES), F32)
    lane_owner = iota((n_owner, LANES), 0).astype(F32)
    place, target = [], []
    for i in range(parts):
        here = stacked[i * n_owner : (i + 1) * n_owner].astype(F32)
        spot = before[i * n_owner : (i + 1) * n_owner] + running
        place.append(jnp.sum(here * spot, axis=0, keepdims=True))
        target.append(jnp.sum(here * lane_owner, axis=0, keepdims=True))
        running = running + totals[i * n_owner : (i + 1) * n_owner]
    place = jnp.concatenate(place, axis=1).astype(I32)
    target = jnp.concatenate(target, axis=1).astype(I32)
    share = place & (n_group - 1)
    entry = place // n_group
    entry = jnp.where(share == me, entry, jnp.where(share == ((me + shift) & (n_group - 1)), entry + cap, -1))
    mine = entry >= 0
    lines = UNITS * cap
    goal = jnp.where(mine, target * lines + entry, -1)
    slot = slot_ref[...]
    high = (slot // BLOCK + 1).astype(F32)
    low = (slot & (BLOCK - 1)).astype(F32)
    width = 16
    row = iota((2 * width, rows), 0)
    values = jnp.where((row & (width - 1)) == entry, jnp.where(row < width, high, low), 0.0).astype(BF16)
    meta = mm_nt(to, values).astype(BF16)
    line = iota((n_owner * META, n_owner), 0)
    peer = iota((n_owner * META, n_owner), 1)
    meta = mm(ones_where(line // META == peer), meta)
    line = iota((n_owner * META, 2 * width), 0) & (META - 1)
    meta = jnp.where(iota((n_owner * META, 2 * width), 1) // width == line, meta, 0.0).astype(BF16)
    column = iota((2 * width, LANES), 0) & (width - 1)
    meta = mm(meta, ones_where(column == iota((2 * width, LANES), 1)))
    out_ref[:, lines * chunks :, :] = meta.reshape(n_owner, META, LANES).astype(BF16)
    select = ones_where(iota((n_owner * lines, rows), 0) == goal)
    total = None
    for i, copy in enumerate(copies[:-1]):
        copy.wait()
        part = mm(select[:, i * step : (i + 1) * step], emb[pl.ds(i * step, step), :])
        total = part if total is None else total + part
    copies[-1].wait()
    last = rows - step
    for k in range(0, chunks, 2):
        part = total[:, k * LANES : (k + 2) * LANES]
        part += mm(select[:, last:], emb[pl.ds(last, step), pl.ds(k * LANES, 2 * LANES)])
        for h in range(2):
            wide[pl.ds(k + h, n_owner * lines, chunks), :] = part[:, h * LANES : (h + 1) * LANES]
    out_ref[:, : lines * chunks, :] = wide[...].reshape(n_owner, lines * chunks, LANES).astype(BF16)


def list_kernel(blocks, pairs_ref, out_ref):
    first, second = pairs_ref[0:1, :], pairs_ref[1:2, :]
    rows, wide = iota((blocks, LANES), 0), iota((LANES, LANES), 0)
    table = mm_nt(ones_where(rows == first), ones_where(wide == second))
    out_ref[...] = table + mm_nt(ones_where(rows == second - blocks), ones_where(wide == first + blocks))


def receive_kernel(n_owner, cap, feat, in_ref, here_ref, there_ref, both_ref, first_ref, wide):
    chunks = feat // LANES
    per_peer = UNITS * cap
    lines = n_owner * per_peer
    size = feat + PAY_META
    wide[...] = in_ref[:, : per_peer * chunks, :].astype(F32).reshape(lines * chunks, LANES)
    meta = in_ref[:, per_peer * chunks :, :].astype(F32).reshape(n_owner * META, LANES).astype(BF16)
    line = iota((lines, n_owner * META), 0)
    source = iota((lines, n_owner * META), 1)
    at_lane = iota((lines, LANES), 1) == lax.rem(iota((lines, LANES), 0), per_peer)
    high = mm(ones_where(source == line // per_peer * META), meta)
    low = mm(ones_where(source == line // per_peer * META + 1), meta)
    ones = jnp.ones((LANES, LANES), BF16)
    high = mm(jnp.where(at_lane, high, 0.0).astype(BF16), ones)
    low = mm(jnp.where(at_lane, low, 0.0).astype(BF16), ones)
    valid = ones_where(high > 0.5)
    later, sooner = iota((lines, lines), 0), iota((lines, lines), 1)
    same = lax.rem(later, per_peer) // cap == lax.rem(sooner, per_peer) // cap
    place = mm(ones_where(jnp.logical_and(sooner < later, same)), valid)
    unit = lax.rem(iota((lines, BLOCK), 0), per_peer) // cap
    here = jnp.logical_and(place == iota((lines, BLOCK), 1).astype(F32), high > 0.5)
    puts = [jnp.logical_and(here, unit == n) for n in range(UNITS)]
    put_one = ones_where(jnp.concatenate(puts, axis=1))
    parts = []
    square = None
    for k in range(chunks):
        part = mm_tn(put_one, wide[pl.ds(k, lines, chunks), :].astype(BF16))
        parts.append(part)
        here = part * part
        square = here if square is None else square + here
    scale = lax.rsqrt(jnp.sum(square, axis=1, keepdims=True) + 1e-06)
    for k in range(chunks):
        piece = (parts[k] * scale).astype(BF16)
        for n in range(UNITS):
            both_ref[pl.ds(n * size + k * BLOCK, BLOCK), :] = piece[n * BLOCK : (n + 1) * BLOCK]
        first_ref[pl.ds(k * BLOCK, BLOCK), :] = piece[:BLOCK]
    row = iota((PAY_META, LANES), 0)
    for n in range(UNITS):
        blocks = jnp.sum(jnp.where(puts[n], high, 0.0), axis=0, keepdims=True) - 1.0
        inner = jnp.sum(jnp.where(puts[n], low, 0.0), axis=0, keepdims=True)
        numbers = jnp.where(row == 0, blocks, jnp.where(row == 1, inner, 0.0)).astype(BF16)
        both_ref[pl.ds(n * size + feat, PAY_META), :] = numbers
        if n == 0:
            first_ref[pl.ds(feat, PAY_META), :] = numbers
    both_ref[pl.ds(UNITS * size, PAY_META), :] = (here_ref[...] + there_ref[...]).astype(BF16)


def rows_of(ref, start, feat):
    return jnp.concatenate([ref[pl.ds(start + k * BLOCK, BLOCK), :] for k in range(feat // LANES)], axis=1)


def numbers_of(ref, start, feat):
    return ref[pl.ds(start + feat, PAY_META), :].astype(F32)[0:2, :].astype(I32)


def stack_rows(places, feat):
    return jnp.concatenate([rows_of(ref, start, feat) for ref, start in places], axis=0)


def stack_numbers(places, feat):
    return jnp.concatenate([numbers_of(ref, start, feat) for ref, start in places], axis=1)


def best_of(left, bias, places, feat, blocks, same=None):
    right = stack_rows(places, feat)
    width = right.shape[0]
    here = ones_where(iota((blocks, width), 0) == stack_numbers(places, feat)[0:1, :])
    scores = mm_nt(left, right) + mm(bias, here)
    if same is not None:
        scores = jnp.where(same, -2.0, scores)
    return jnp.max(scores, axis=0, keepdims=True)


def bias_of(penalty, marks):
    picked = ones_where(iota((LANES, marks.shape[1]), 0) == marks)
    return lax.dot_general(picked, penalty, (((0,), (1,)), ((), ())), preferred_element_type=F32).astype(BF16)


def slot_table(best, numbers, blocks):
    total = best.shape[1]
    best = jnp.maximum(best, -2.0)
    spread = iota((blocks, total), 0) == numbers[0:1, :]
    inner = ones_where(iota((BLOCK, total), 0) == numbers[1:2, :])
    filled = mm_nt(ones_where(spread), inner)
    result = jnp.zeros((blocks, BLOCK), F32)
    rest = best
    for _ in range(3):
        piece = rest.astype(BF16).astype(F32)
        rest = rest - piece
        result += mm_nt(jnp.where(spread, piece, 0.0).astype(BF16), inner)
    return jnp.where(filled > 0.5, result, -2.0)


def first_score_kernel(blocks, feat, own_ref, twin_ref, back_ref, next_ref, left_ref, right_ref, out_ref, bias_ref):
    size = feat + PAY_META
    paired = own_ref[pl.ds(UNITS * size, PAY_META), :].astype(F32) + twin_ref[pl.ds(UNITS * size, PAY_META), :].astype(F32)
    penalty = jnp.where(paired > 0.5, 0.0, -4.0).astype(BF16)
    across = [(left_ref, 0), (right_ref, 0), (left_ref, size), (right_ref, size)]
    marks = stack_numbers(across, feat)[0:1, :]
    odd = lax.axis_index("owner") & 1
    marks += 2 * blocks * jnp.where((iota(marks.shape, 1) & BLOCK) == 0, 1 - odd, odd)
    across_bias = bias_of(penalty, marks)
    bias_ref[...] = across_bias
    across_rows = stack_rows(across, feat)
    inside = [(next_ref, 0), (back_ref, 0), (own_ref, 0), (twin_ref, 0), (own_ref, size), (twin_ref, size)]
    inside_bias = bias_of(penalty, stack_numbers(inside, feat)[0:1, :] + blocks)
    inside_rows = stack_rows(inside, feat)
    row, lane = iota((5 * BLOCK, 2 * BLOCK), 0), iota((5 * BLOCK, 2 * BLOCK), 1)
    groups = [
        ([(own_ref, 0), (twin_ref, 0)], 4, 1, 6, row == lane + BLOCK),
        ([(own_ref, size), (twin_ref, size)], 2, 0, 3, None),
        ([(back_ref, 0), (next_ref, 0)], 4, 2, 6, None),
    ]
    best, numbers = [], []
    for places, count, low, high, equal in groups:
        part = slice(low * BLOCK, high * BLOCK)
        outer = slice(0, count * BLOCK)
        one = best_of(across_rows[outer], across_bias[outer], places, feat, blocks)
        two = best_of(inside_rows[part], inside_bias[part], places, feat, blocks, equal)
        best.append(jnp.maximum(one, two))
        numbers.append(stack_numbers(places, feat))
    out_ref[...] = slot_table(jnp.concatenate(best, axis=1), jnp.concatenate(numbers, axis=1), blocks)


def second_score_kernel(blocks, feat, table_ref, bias_ref, left_ref, right_ref, back_ref, late_ref, out_ref):
    size = feat + PAY_META
    across_rows = stack_rows([(left_ref, 0), (right_ref, 0), (left_ref, size), (right_ref, size)], feat)
    across_bias = bias_ref[...]
    best, numbers = [], []
    for places, count in (([(back_ref, size), (late_ref, size)], 2), ([(late_ref, 0), (late_ref, 2 * size)], 4)):
        outer = slice(0, count * BLOCK)
        best.append(best_of(across_rows[outer], across_bias[outer], places, feat, blocks))
        numbers.append(stack_numbers(places, feat))
    table = slot_table(jnp.concatenate(best, axis=1), jnp.concatenate(numbers, axis=1), blocks)
    table = jnp.maximum(table_ref[...], table)
    for b in range(blocks):
        out_ref[b] = jnp.broadcast_to(table[b : b + 1, :], (8, BLOCK))


def vmem():
    return pl.BlockSpec(memory_space=pltpu.VMEM)


def far():
    return pl.BlockSpec(memory_space=pltpu.HBM)


PARAMS = pltpu.CompilerParams(vmem_limit_bytes=48 * 1024 * 1024)


def cost(flops, nbytes):
    return pl.CostEstimate(flops=flops, bytes_accessed=nbytes, transcendentals=0)


def on_device(embeddings, cluster_of, cluster_owner, slot_of, pairs):
    n_owner = lax.axis_size("owner")
    n_group = lax.axis_size("group")
    rows, feat = embeddings.shape
    chunks = feat // LANES
    cap = 3 * rows // (2 * n_owner * n_group)
    lines = UNITS * cap
    pieces = 4
    size = feat + PAY_META
    outgoing = pl.pallas_call(
        lambda *refs: send_kernel(n_owner, n_group, cap, 6, pieces, *refs),
        out_shape=jax.ShapeDtypeStruct((n_owner, lines * chunks + META, LANES), BF16),
        in_specs=[far()] * 4,
        out_specs=vmem(),
        scratch_shapes=[
            pltpu.VMEM((rows, feat), BF16),
            pltpu.VMEM((n_owner * lines * chunks, LANES), F32),
            pltpu.VMEM((1, rows), I32),
            pltpu.VMEM((1, n_owner), I32),
            pltpu.VMEM((1, rows), I32),
            pltpu.SemaphoreType.DMA((pieces + 3,)),
        ],
        compiler_params=PARAMS,
        name="send_rows",
    )(
        *[
            pltpu.with_memory_space_constraint(x, pltpu.HBM)
            for x in (cluster_of.reshape(1, rows), cluster_owner.reshape(1, n_owner), slot_of.reshape(1, rows), embeddings)
        ]
    )
    arrived = lax.all_to_all(outgoing, "owner", split_axis=0, concat_axis=0, tiled=True)
    swap = [(i, i ^ 1) for i in range(n_group)]

    def along_y(x, partner):
        return lax.ppermute(x, "group", [(i, 2 * (partner(i // 2) % (n_group // 2)) + i % 2) for i in range(n_group)])

    def along_owner(x, partner):
        return lax.ppermute(x, "owner", [(i, partner(i) % n_owner) for i in range(n_owner)])

    entries = pairs.reshape(-1, 2)
    listed = jnp.pad(entries.T, ((0, 0), (0, LANES - entries.shape[0])), constant_values=-1)
    here = pl.pallas_call(
        lambda *refs: list_kernel(n_group, *refs),
        out_shape=jax.ShapeDtypeStruct((n_group, LANES), F32),
        in_specs=[vmem()],
        out_specs=vmem(),
        compiler_params=PARAMS,
        name="list_table",
    )(listed)
    there = along_y(here, lambda y: y ^ 1)
    here = here + there
    there = along_y(here, lambda y: y ^ 2)
    here = here + there
    there = along_y(here, lambda y: y ^ 4)
    both, first = pl.pallas_call(
        lambda *refs: receive_kernel(n_owner, cap, feat, *refs),
        out_shape=[
            jax.ShapeDtypeStruct((UNITS * size + PAY_META, LANES), BF16),
            jax.ShapeDtypeStruct((size, LANES), BF16),
        ],
        in_specs=[vmem()] * 3,
        out_specs=[vmem()] * 2,
        scratch_shapes=[pltpu.VMEM((n_owner * lines * chunks, LANES), F32)],
        compiler_params=PARAMS,
        name="unit_rows",
    )(arrived, here, there)
    twin = lax.ppermute(both, "group", swap)
    following, back = along_y(first, lambda y: y - 1), along_y(both, lambda y: y + 1)
    left, right = along_owner(both, lambda o: o ^ 1), along_owner(both, lambda o: o + 2 * (o & 1) - 1)
    following, right, back, left = lax.optimization_barrier((following, right, back, left))
    late = lax.ppermute(jnp.concatenate([back[: 2 * size], following], axis=0), "group", swap)
    table, bias = pl.pallas_call(
        lambda *refs: first_score_kernel(n_group, feat, *refs),
        out_shape=[
            jax.ShapeDtypeStruct((n_group, BLOCK), F32),
            jax.ShapeDtypeStruct((4 * BLOCK, n_group), BF16),
        ],
        in_specs=[vmem()] * 6,
        out_specs=[vmem()] * 2,
        compiler_params=PARAMS,
        cost_estimate=cost(3 * 10**9, 4 * 10**6),
        name="score_rows",
    )(both, twin, back, following, left, right)
    table = pl.pallas_call(
        lambda *refs: second_score_kernel(n_group, feat, *refs),
        out_shape=jax.ShapeDtypeStruct((n_group, 8, BLOCK), F32),
        in_specs=[vmem()] * 6,
        out_specs=vmem(),
        compiler_params=PARAMS,
        cost_estimate=cost(5 * 10**8, 2 * 10**6),
        name="score_rest",
    )(table, bias, left, right, back, late)
    shares = lax.all_to_all(table, "group", split_axis=0, concat_axis=0, tiled=True)
    return jnp.max(shares[:, :1], axis=0)


def solution(mesh):
    placed = (P("owner", None), P("owner"), P(), P("owner"), P("owner", "group", None, None))
    return jax.shard_map(
        on_device, mesh=mesh, in_specs=placed, out_specs=P("owner", "group"), check_vma=False
    )
```

```python
import jax
import jax.numpy as jnp
from jax import lax
from jax.experimental import pallas as pl
from jax.experimental.pallas import tpu as pltpu
from jax.sharding import PartitionSpec as P

BLOCK = 128
LANES = 128
META = 8
PAY_META = 16
UNITS = 2
BF16 = jnp.bfloat16
F32 = jnp.float32
I32 = jnp.int32


def iota(shape, dim):
    return lax.broadcasted_iota(I32, shape, dim)


def ones_where(mask):
    return jnp.where(mask, 1.0, 0.0).astype(BF16)


def mm(a, b):
    return jnp.dot(a, b, preferred_element_type=F32)


def mm_nt(a, b):
    return lax.dot_general(a, b, (((1,), (1,)), ((), ())), preferred_element_type=F32)


def mm_tn(a, b):
    return lax.dot_general(a, b, (((0,), (0,)), ((), ())), preferred_element_type=F32)


def send_kernel(n_owner, n_group, cap, shift, pieces, cluster_hbm, owner_hbm, slot_hbm, emb_ref, out_ref, emb, wide, cluster_ref, owner_ref, slot_ref, sems):
    rows, feat = emb.shape
    chunks = feat // LANES
    step = rows // pieces
    small = [
        pltpu.make_async_copy(source, goal, sems.at[pieces + i])
        for i, (source, goal) in enumerate(
            ((cluster_hbm, cluster_ref), (owner_hbm, owner_ref), (slot_hbm, slot_ref))
        )
    ]
    copies = [
        pltpu.make_async_copy(emb_ref.at[pl.ds(i * step, step)], emb.at[pl.ds(i * step, step)], sems.at[i])
        for i in range(pieces)
    ]
    for copy in small + copies:
        copy.start()
    for copy in small:
        copy.wait()
    me = lax.axis_index("group")
    picked = ones_where(iota((n_owner, rows), 0) == cluster_ref[...])
    table = ones_where(iota((n_owner, n_owner), 0) == owner_ref[...])
    to = mm(table, picked).astype(BF16)
    parts = rows // LANES
    stacked = jnp.concatenate([to[:, i * LANES : (i + 1) * LANES] for i in range(parts)], axis=0)
    before = mm(stacked, ones_where(iota((LANES, LANES), 0) < iota((LANES, LANES), 1)))
    totals = mm(stacked, jnp.ones((LANES, LANES), BF16))
    running = jnp.zeros((n_owner, LANES), F32)
    lane_owner = iota((n_owner, LANES), 0).astype(F32)
    place, target = [], []
    for i in range(parts):
        here = stacked[i * n_owner : (i + 1) * n_owner].astype(F32)
        spot = before[i * n_owner : (i + 1) * n_owner] + running
        place.append(jnp.sum(here * spot, axis=0, keepdims=True))
        target.append(jnp.sum(here * lane_owner, axis=0, keepdims=True))
        running = running + totals[i * n_owner : (i + 1) * n_owner]
    place = jnp.concatenate(place, axis=1).astype(I32)
    target = jnp.concatenate(target, axis=1).astype(I32)
    share = place & (n_group - 1)
    entry = place // n_group
    entry = jnp.where(share == me, entry, jnp.where(share == ((me + shift) & (n_group - 1)), entry + cap, -1))
    mine = entry >= 0
    lines = UNITS * cap
    goal = jnp.where(mine, target * lines + entry, -1)
    slot = slot_ref[...]
    high = (slot // BLOCK + 1).astype(F32)
    low = (slot & (BLOCK - 1)).astype(F32)
    width = 16
    row = iota((2 * width, rows), 0)
    values = jnp.where((row & (width - 1)) == entry, jnp.where(row < width, high, low), 0.0).astype(BF16)
    meta = mm_nt(to, values).astype(BF16)
    line = iota((n_owner * META, n_owner), 0)
    peer = iota((n_owner * META, n_owner), 1)
    meta = mm(ones_where(line // META == peer), meta)
    line = iota((n_owner * META, 2 * width), 0) & (META - 1)
    meta = jnp.where(iota((n_owner * META, 2 * width), 1) // width == line, meta, 0.0).astype(BF16)
    column = iota((2 * width, LANES), 0) & (width - 1)
    meta = mm(meta, ones_where(column == iota((2 * width, LANES), 1)))
    out_ref[:, lines * chunks :, :] = meta.reshape(n_owner, META, LANES).astype(BF16)
    middle = n_owner * lines // 2
    line = (iota((n_owner * lines, 1), 0) - middle).astype(F32).astype(BF16)
    goal = jnp.where(mine, goal - middle, middle).astype(F32).astype(BF16)
    select = jnp.where(line == goal, jnp.ones((), BF16), jnp.zeros((), BF16))
    total = None
    for i, copy in enumerate(copies[:-1]):
        copy.wait()
        part = mm(select[:, i * step : (i + 1) * step], emb[pl.ds(i * step, step), :])
        total = part if total is None else total + part
    copies[-1].wait()
    last = rows - step
    for k in range(0, chunks, 2):
        part = total[:, k * LANES : (k + 2) * LANES]
        part += mm(select[:, last:], emb[pl.ds(last, step), pl.ds(k * LANES, 2 * LANES)])
        for h in range(2):
            wide[pl.ds(k + h, n_owner * lines, chunks), :] = part[:, h * LANES : (h + 1) * LANES]
    out_ref[:, : lines * chunks, :] = wide[...].reshape(n_owner, lines * chunks, LANES).astype(BF16)


def list_kernel(blocks, pairs_ref, out_ref):
    first, second = pairs_ref[0:1, :], pairs_ref[1:2, :]
    rows, wide = iota((blocks, LANES), 0), iota((LANES, LANES), 0)
    table = mm_nt(ones_where(rows == first), ones_where(wide == second))
    out_ref[...] = table + mm_nt(ones_where(rows == second - blocks), ones_where(wide == first + blocks))


def receive_kernel(n_owner, cap, feat, in_ref, here_ref, there_ref, both_ref, first_ref, wide):
    chunks = feat // LANES
    per_peer = UNITS * cap
    lines = n_owner * per_peer
    size = feat + PAY_META
    wide[...] = in_ref[:, : per_peer * chunks, :].astype(F32).reshape(lines * chunks, LANES)
    meta = in_ref[:, per_peer * chunks :, :].astype(F32).reshape(n_owner * META, LANES).astype(BF16)
    line = iota((lines, n_owner * META), 0)
    source = iota((lines, n_owner * META), 1)
    at_lane = iota((lines, LANES), 1) == lax.rem(iota((lines, LANES), 0), per_peer)
    high = mm(ones_where(source == line // per_peer * META), meta)
    low = mm(ones_where(source == line // per_peer * META + 1), meta)
    ones = jnp.ones((LANES, LANES), BF16)
    high = mm(jnp.where(at_lane, high, 0.0).astype(BF16), ones)
    low = mm(jnp.where(at_lane, low, 0.0).astype(BF16), ones)
    valid = ones_where(high > 0.5)
    later, sooner = iota((lines, lines), 0), iota((lines, lines), 1)
    same = lax.rem(later, per_peer) // cap == lax.rem(sooner, per_peer) // cap
    place = mm(ones_where(jnp.logical_and(sooner < later, same)), valid)
    unit = lax.rem(iota((lines, BLOCK), 0), per_peer) // cap
    here = jnp.logical_and(place == iota((lines, BLOCK), 1).astype(F32), high > 0.5)
    puts = [jnp.logical_and(here, unit == n) for n in range(UNITS)]
    put_one = ones_where(jnp.concatenate(puts, axis=1))
    parts = []
    square = None
    for k in range(chunks):
        part = mm_tn(put_one, wide[pl.ds(k, lines, chunks), :].astype(BF16))
        parts.append(part)
        here = part * part
        square = here if square is None else square + here
    scale = lax.rsqrt(jnp.sum(square, axis=1, keepdims=True) + 1e-06)
    for k in range(chunks):
        piece = (parts[k] * scale).astype(BF16)
        for n in range(UNITS):
            both_ref[pl.ds(n * size + k * BLOCK, BLOCK), :] = piece[n * BLOCK : (n + 1) * BLOCK]
        first_ref[pl.ds(k * BLOCK, BLOCK), :] = piece[:BLOCK]
    row = iota((PAY_META, LANES), 0)
    for n in range(UNITS):
        blocks = jnp.sum(jnp.where(puts[n], high, 0.0), axis=0, keepdims=True) - 1.0
        inner = jnp.sum(jnp.where(puts[n], low, 0.0), axis=0, keepdims=True)
        numbers = jnp.where(row == 0, blocks, jnp.where(row == 1, inner, 0.0)).astype(BF16)
        both_ref[pl.ds(n * size + feat, PAY_META), :] = numbers
        if n == 0:
            first_ref[pl.ds(feat, PAY_META), :] = numbers
    both_ref[pl.ds(UNITS * size, PAY_META), :] = (here_ref[...] + there_ref[...]).astype(BF16)


def rows_of(ref, start, feat):
    return jnp.concatenate([ref[pl.ds(start + k * BLOCK, BLOCK), :] for k in range(feat // LANES)], axis=1)


def numbers_of(ref, start, feat):
    return ref[pl.ds(start + feat, PAY_META), :].astype(F32)[0:2, :].astype(I32)


def stack_rows(places, feat):
    return jnp.concatenate([rows_of(ref, start, feat) for ref, start in places], axis=0)


def stack_numbers(places, feat):
    return jnp.concatenate([numbers_of(ref, start, feat) for ref, start in places], axis=1)


def best_of(left, bias, places, feat, blocks, same=None):
    right = stack_rows(places, feat)
    width = right.shape[0]
    here = ones_where(iota((blocks, width), 0) == stack_numbers(places, feat)[0:1, :])
    scores = mm_nt(left, right) + mm(bias, here)
    if same is not None:
        scores = jnp.where(same, -2.0, scores)
    return jnp.max(scores, axis=0, keepdims=True)


def bias_of(penalty, marks):
    picked = ones_where(iota((LANES, marks.shape[1]), 0) == marks)
    return lax.dot_general(picked, penalty, (((0,), (1,)), ((), ())), preferred_element_type=F32).astype(BF16)


def slot_table(best, numbers, blocks):
    total = best.shape[1]
    best = jnp.maximum(best, -2.0)
    spread = iota((blocks, total), 0) == numbers[0:1, :]
    inner = ones_where(iota((BLOCK, total), 0) == numbers[1:2, :])
    filled = mm_nt(ones_where(spread), inner)
    result = jnp.zeros((blocks, BLOCK), F32)
    rest = best
    for _ in range(3):
        piece = rest.astype(BF16).astype(F32)
        rest = rest - piece
        result += mm_nt(jnp.where(spread, piece, 0.0).astype(BF16), inner)
    return jnp.where(filled > 0.5, result, -2.0)


def first_score_kernel(blocks, feat, own_ref, twin_ref, back_ref, next_ref, left_ref, right_ref, out_ref, bias_ref):
    size = feat + PAY_META
    paired = own_ref[pl.ds(UNITS * size, PAY_META), :].astype(F32) + twin_ref[pl.ds(UNITS * size, PAY_META), :].astype(F32)
    penalty = jnp.where(paired > 0.5, 0.0, -4.0).astype(BF16)
    across = [(left_ref, 0), (right_ref, 0), (left_ref, size), (right_ref, size)]
    marks = stack_numbers(across, feat)[0:1, :]
    odd = lax.axis_index("owner") & 1
    marks += 2 * blocks * jnp.where((iota(marks.shape, 1) & BLOCK) == 0, 1 - odd, odd)
    across_bias = bias_of(penalty, marks)
    bias_ref[...] = across_bias
    across_rows = stack_rows(across, feat)
    inside = [(twin_ref, size), (next_ref, 0), (back_ref, size), (own_ref, 0), (own_ref, size), (twin_ref, size)]
    inside_bias = bias_of(penalty, stack_numbers(inside, feat)[0:1, :] + blocks)
    inside_rows = stack_rows(inside, feat)
    row, lane = iota((4 * BLOCK, 2 * BLOCK), 0), iota((4 * BLOCK, 2 * BLOCK), 1)
    same = jnp.logical_and(row - 3 * BLOCK == lane, lane < BLOCK)
    groups = [
        ([(own_ref, 0), (twin_ref, 0)], 4, 0, 2, None),
        ([(own_ref, size), (twin_ref, size)], 2, 1, 5, same),
        ([(back_ref, 0), (next_ref, 0)], 4, 4, 6, None),
    ]
    best, numbers = [], []
    for places, count, low, high, equal in groups:
        part = slice(low * BLOCK, high * BLOCK)
        outer = slice(0, count * BLOCK)
        one = best_of(across_rows[outer], across_bias[outer], places, feat, blocks)
        two = best_of(inside_rows[part], inside_bias[part], places, feat, blocks, equal)
        best.append(jnp.maximum(one, two))
        numbers.append(stack_numbers(places, feat))
    out_ref[...] = slot_table(jnp.concatenate(best, axis=1), jnp.concatenate(numbers, axis=1), blocks)


def second_score_kernel(blocks, feat, table_ref, bias_ref, left_ref, right_ref, back_ref, late_ref, out_ref):
    size = feat + PAY_META
    across_rows = stack_rows([(left_ref, 0), (right_ref, 0), (left_ref, size), (right_ref, size)], feat)
    across_bias = bias_ref[...]
    best, numbers = [], []
    for places, count in (([(back_ref, size), (late_ref, size)], 2), ([(late_ref, 0), (late_ref, 2 * size)], 4)):
        outer = slice(0, count * BLOCK)
        best.append(best_of(across_rows[outer], across_bias[outer], places, feat, blocks))
        numbers.append(stack_numbers(places, feat))
    table = slot_table(jnp.concatenate(best, axis=1), jnp.concatenate(numbers, axis=1), blocks)
    table = jnp.maximum(table_ref[...], table)
    for b in range(blocks):
        out_ref[b] = jnp.broadcast_to(table[b : b + 1, :], (8, BLOCK))


def vmem():
    return pl.BlockSpec(memory_space=pltpu.VMEM)


def far():
    return pl.BlockSpec(memory_space=pltpu.HBM)


PARAMS = pltpu.CompilerParams(vmem_limit_bytes=48 * 1024 * 1024)


def cost(flops, nbytes):
    return pl.CostEstimate(flops=flops, bytes_accessed=nbytes, transcendentals=0)


def on_device(embeddings, cluster_of, cluster_owner, slot_of, pairs):
    n_owner = lax.axis_size("owner")
    n_group = lax.axis_size("group")
    rows, feat = embeddings.shape
    chunks = feat // LANES
    cap = 3 * rows // (2 * n_owner * n_group)
    lines = UNITS * cap
    pieces = 2
    size = feat + PAY_META
    outgoing = pl.pallas_call(
        lambda *refs: send_kernel(n_owner, n_group, cap, 6, pieces, *refs),
        out_shape=jax.ShapeDtypeStruct((n_owner, lines * chunks + META, LANES), BF16),
        in_specs=[far()] * 4,
        out_specs=vmem(),
        scratch_shapes=[
            pltpu.VMEM((rows, feat), BF16),
            pltpu.VMEM((n_owner * lines * chunks, LANES), F32),
            pltpu.VMEM((1, rows), I32),
            pltpu.VMEM((1, n_owner), I32),
            pltpu.VMEM((1, rows), I32),
            pltpu.SemaphoreType.DMA((pieces + 3,)),
        ],
        compiler_params=PARAMS,
        name="send_rows",
    )(
        *[
            pltpu.with_memory_space_constraint(x, pltpu.HBM)
            for x in (cluster_of.reshape(1, rows), cluster_owner.reshape(1, n_owner), slot_of.reshape(1, rows), embeddings)
        ]
    )
    arrived = lax.all_to_all(outgoing, "owner", split_axis=0, concat_axis=0, tiled=True)
    swap = [(i, i ^ 1) for i in range(n_group)]

    def along_y(x, partner):
        return lax.ppermute(x, "group", [(i, 2 * (partner(i // 2) % (n_group // 2)) + i % 2) for i in range(n_group)])

    def along_owner(x, partner):
        return lax.ppermute(x, "owner", [(i, partner(i) % n_owner) for i in range(n_owner)])

    entries = pairs.reshape(-1, 2)
    listed = jnp.pad(entries.T, ((0, 0), (0, LANES - entries.shape[0])), constant_values=-1)
    here = pl.pallas_call(
        lambda *refs: list_kernel(n_group, *refs),
        out_shape=jax.ShapeDtypeStruct((n_group, LANES), F32),
        in_specs=[vmem()],
        out_specs=vmem(),
        compiler_params=PARAMS,
        name="list_table",
    )(listed)
    there = along_y(here, lambda y: y ^ 1)
    here = here + there
    there = along_y(here, lambda y: y ^ 2)
    here = here + there
    there = along_y(here, lambda y: y ^ 4)
    both, first = pl.pallas_call(
        lambda *refs: receive_kernel(n_owner, cap, feat, *refs),
        out_shape=[
            jax.ShapeDtypeStruct((UNITS * size + PAY_META, LANES), BF16),
            jax.ShapeDtypeStruct((size, LANES), BF16),
        ],
        in_specs=[vmem()] * 3,
        out_specs=[vmem()] * 2,
        scratch_shapes=[pltpu.VMEM((n_owner * lines * chunks, LANES), F32)],
        compiler_params=PARAMS,
        name="unit_rows",
    )(arrived, here, there)
    twin = lax.ppermute(both, "group", swap)
    following, back = along_y(first, lambda y: y - 1), along_y(both, lambda y: y + 1)
    left, right = along_owner(both, lambda o: o ^ 1), along_owner(both, lambda o: o + 2 * (o & 1) - 1)
    following, right, back, left = lax.optimization_barrier((following, right, back, left))
    late = lax.ppermute(jnp.concatenate([back[: 2 * size], following], axis=0), "group", swap)
    table, bias = pl.pallas_call(
        lambda *refs: first_score_kernel(n_group, feat, *refs),
        out_shape=[
            jax.ShapeDtypeStruct((n_group, BLOCK), F32),
            jax.ShapeDtypeStruct((4 * BLOCK, n_group), BF16),
        ],
        in_specs=[vmem()] * 6,
        out_specs=[vmem()] * 2,
        compiler_params=PARAMS,
        cost_estimate=cost(3 * 10**9, 4 * 10**6),
        name="score_rows",
    )(both, twin, back, following, left, right)
    table = pl.pallas_call(
        lambda *refs: second_score_kernel(n_group, feat, *refs),
        out_shape=jax.ShapeDtypeStruct((n_group, 8, BLOCK), F32),
        in_specs=[vmem()] * 6,
        out_specs=vmem(),
        compiler_params=PARAMS,
        cost_estimate=cost(5 * 10**8, 2 * 10**6),
        name="score_rest",
    )(table, bias, left, right, back, late)
    shares = lax.all_to_all(table, "group", split_axis=0, concat_axis=0, tiled=True)
    return jnp.max(shares[:, :1], axis=0)


def solution(mesh):
    placed = (P("owner", None), P("owner"), P(), P("owner"), P("owner", "group", None, None))
    return jax.shard_map(
        on_device, mesh=mesh, in_specs=placed, out_specs=P("owner", "group"), check_vma=False
    )
```

```python
import jax
import jax.numpy as jnp
from jax import lax
from jax.experimental import pallas as pl
from jax.experimental.pallas import tpu as pltpu
from jax.sharding import PartitionSpec as P

BLOCK = 128
LANES = 128
META = 8
PAY_META = 16
UNITS = 2
BF16 = jnp.bfloat16
F32 = jnp.float32
I32 = jnp.int32


def iota(shape, dim):
    return lax.broadcasted_iota(I32, shape, dim)


def ones_where(mask):
    return jnp.where(mask, 1.0, 0.0).astype(BF16)


def mm(a, b):
    return jnp.dot(a, b, preferred_element_type=F32)


def mm_nt(a, b):
    return lax.dot_general(a, b, (((1,), (1,)), ((), ())), preferred_element_type=F32)


def mm_tn(a, b):
    return lax.dot_general(a, b, (((0,), (0,)), ((), ())), preferred_element_type=F32)


def send_kernel(n_owner, n_group, cap, shift, pieces, cluster_hbm, owner_hbm, slot_hbm, emb_ref, out_ref, emb, wide, cluster_ref, owner_ref, slot_ref, sems):
    rows, feat = emb.shape
    chunks = feat // LANES
    step = rows // pieces
    small = [
        pltpu.make_async_copy(source, goal, sems.at[pieces + i])
        for i, (source, goal) in enumerate(
            ((cluster_hbm, cluster_ref), (owner_hbm, owner_ref), (slot_hbm, slot_ref))
        )
    ]
    copies = [
        pltpu.make_async_copy(emb_ref.at[pl.ds(i * step, step)], emb.at[pl.ds(i * step, step)], sems.at[i])
        for i in range(pieces)
    ]
    for copy in small + copies:
        copy.start()
    for copy in small:
        copy.wait()
    me = lax.axis_index("group")
    picked = ones_where(iota((n_owner, rows), 0) == cluster_ref[...])
    table = ones_where(iota((n_owner, n_owner), 0) == owner_ref[...])
    to = mm(table, picked).astype(BF16)
    parts = rows // LANES
    stacked = jnp.concatenate([to[:, i * LANES : (i + 1) * LANES] for i in range(parts)], axis=0)
    before = mm(stacked, ones_where(iota((LANES, LANES), 0) < iota((LANES, LANES), 1)))
    totals = mm(stacked, jnp.ones((LANES, LANES), BF16))
    running = jnp.zeros((n_owner, LANES), F32)
    lane_owner = iota((n_owner, LANES), 0).astype(F32)
    place, target = [], []
    for i in range(parts):
        here = stacked[i * n_owner : (i + 1) * n_owner].astype(F32)
        spot = before[i * n_owner : (i + 1) * n_owner] + running
        place.append(jnp.sum(here * spot, axis=0, keepdims=True))
        target.append(jnp.sum(here * lane_owner, axis=0, keepdims=True))
        running = running + totals[i * n_owner : (i + 1) * n_owner]
    place = jnp.concatenate(place, axis=1).astype(I32)
    target = jnp.concatenate(target, axis=1).astype(I32)
    share = place & (n_group - 1)
    entry = place // n_group
    entry = jnp.where(share == me, entry, jnp.where(share == ((me + shift) & (n_group - 1)), entry + cap, -1))
    mine = entry >= 0
    lines = UNITS * cap
    goal = jnp.where(mine, target * lines + entry, -1)
    slot = slot_ref[...]
    high = (slot // BLOCK + 1).astype(F32)
    low = (slot & (BLOCK - 1)).astype(F32)
    width = 16
    row = iota((2 * width, rows), 0)
    values = jnp.where((row & (width - 1)) == entry, jnp.where(row < width, high, low), 0.0).astype(BF16)
    meta = mm_nt(to, values).astype(BF16)
    line = iota((n_owner * META, n_owner), 0)
    peer = iota((n_owner * META, n_owner), 1)
    meta = mm(ones_where(line // META == peer), meta)
    line = iota((n_owner * META, 2 * width), 0) & (META - 1)
    meta = jnp.where(iota((n_owner * META, 2 * width), 1) // width == line, meta, 0.0).astype(BF16)
    column = iota((2 * width, LANES), 0) & (width - 1)
    meta = mm(meta, ones_where(column == iota((2 * width, LANES), 1)))
    out_ref[:, lines * chunks :, :] = meta.reshape(n_owner, META, LANES).astype(BF16)
    middle = n_owner * lines // 2
    line = (iota((n_owner * lines, 1), 0) - middle).astype(F32).astype(BF16)
    goal = jnp.where(mine, goal - middle, middle).astype(F32).astype(BF16)
    select = jnp.where(line == goal, jnp.ones((), BF16), jnp.zeros((), BF16))
    total = None
    for i, copy in enumerate(copies[:-1]):
        copy.wait()
        part = mm(select[:, i * step : (i + 1) * step], emb[pl.ds(i * step, step), :])
        total = part if total is None else total + part
    copies[-1].wait()
    last = rows - step
    for k in range(0, chunks, 2):
        part = total[:, k * LANES : (k + 2) * LANES]
        part += mm(select[:, last:], emb[pl.ds(last, step), pl.ds(k * LANES, 2 * LANES)])
        for h in range(2):
            wide[pl.ds(k + h, n_owner * lines, chunks), :] = part[:, h * LANES : (h + 1) * LANES]
    out_ref[:, : lines * chunks, :] = wide[...].reshape(n_owner, lines * chunks, LANES).astype(BF16)


def list_kernel(blocks, pairs_ref, out_ref):
    first, second = pairs_ref[0:1, :], pairs_ref[1:2, :]
    rows, wide = iota((blocks, LANES), 0), iota((LANES, LANES), 0)
    table = mm_nt(ones_where(rows == first), ones_where(wide == second))
    out_ref[...] = table + mm_nt(ones_where(rows == second - blocks), ones_where(wide == first + blocks))


def receive_kernel(n_owner, cap, feat, in_ref, here_ref, there_ref, both_ref, first_ref, wide):
    chunks = feat // LANES
    per_peer = UNITS * cap
    lines = n_owner * per_peer
    size = feat + PAY_META
    wide[...] = in_ref[:, : per_peer * chunks, :].astype(F32).reshape(lines * chunks, LANES)
    meta = in_ref[:, per_peer * chunks :, :].astype(F32).reshape(n_owner * META, LANES).astype(BF16)
    line = iota((lines, n_owner * META), 0)
    source = iota((lines, n_owner * META), 1)
    at_lane = iota((lines, LANES), 1) == lax.rem(iota((lines, LANES), 0), per_peer)
    high = mm(ones_where(source == line // per_peer * META), meta)
    low = mm(ones_where(source == line // per_peer * META + 1), meta)
    ones = jnp.ones((LANES, LANES), BF16)
    high = mm(jnp.where(at_lane, high, 0.0).astype(BF16), ones)
    low = mm(jnp.where(at_lane, low, 0.0).astype(BF16), ones)
    valid = ones_where(high > 0.5)
    later, sooner = iota((lines, lines), 0), iota((lines, lines), 1)
    same = lax.rem(later, per_peer) // cap == lax.rem(sooner, per_peer) // cap
    place = mm(ones_where(jnp.logical_and(sooner < later, same)), valid)
    unit = lax.rem(iota((lines, BLOCK), 0), per_peer) // cap
    here = jnp.logical_and(place == iota((lines, BLOCK), 1).astype(F32), high > 0.5)
    puts = [jnp.logical_and(here, unit == n) for n in range(UNITS)]
    put_one = ones_where(jnp.concatenate(puts, axis=1))
    parts = []
    square = None
    for k in range(chunks):
        part = mm_tn(put_one, wide[pl.ds(k, lines, chunks), :].astype(BF16))
        parts.append(part)
        here = part * part
        square = here if square is None else square + here
    scale = lax.rsqrt(jnp.sum(square, axis=1, keepdims=True) + 1e-06)
    for k in range(chunks):
        piece = (parts[k] * scale).astype(BF16)
        for n in range(UNITS):
            both_ref[pl.ds(n * size + k * BLOCK, BLOCK), :] = piece[n * BLOCK : (n + 1) * BLOCK]
        first_ref[pl.ds(k * BLOCK, BLOCK), :] = piece[:BLOCK]
    row = iota((PAY_META, LANES), 0)
    for n in range(UNITS):
        blocks = jnp.sum(jnp.where(puts[n], high, 0.0), axis=0, keepdims=True) - 1.0
        inner = jnp.sum(jnp.where(puts[n], low, 0.0), axis=0, keepdims=True)
        numbers = jnp.where(row == 0, blocks, jnp.where(row == 1, inner, 0.0)).astype(BF16)
        both_ref[pl.ds(n * size + feat, PAY_META), :] = numbers
        if n == 0:
            first_ref[pl.ds(feat, PAY_META), :] = numbers
    both_ref[pl.ds(UNITS * size, PAY_META), :] = (here_ref[...] + there_ref[...]).astype(BF16)


def rows_of(ref, start, feat):
    return jnp.concatenate([ref[pl.ds(start + k * BLOCK, BLOCK), :] for k in range(feat // LANES)], axis=1)


def numbers_of(ref, start, feat):
    return ref[pl.ds(start + feat, PAY_META), :].astype(F32)[0:2, :].astype(I32)


def stack_rows(places, feat):
    return jnp.concatenate([rows_of(ref, start, feat) for ref, start in places], axis=0)


def stack_numbers(places, feat):
    return jnp.concatenate([numbers_of(ref, start, feat) for ref, start in places], axis=1)


def best_of(left, bias, places, feat, blocks, same=None):
    right = stack_rows(places, feat)
    width = right.shape[0]
    here = ones_where(iota((blocks, width), 0) == stack_numbers(places, feat)[0:1, :])
    scores = mm_nt(left, right) + mm(bias, here)
    if same is not None:
        scores = jnp.where(same, -2.0, scores)
    return jnp.max(scores, axis=0, keepdims=True)


def bias_of(penalty, marks):
    picked = ones_where(iota((LANES, marks.shape[1]), 0) == marks)
    return lax.dot_general(picked, penalty, (((0,), (1,)), ((), ())), preferred_element_type=F32).astype(BF16)


def slot_table(best, numbers, blocks):
    total = best.shape[1]
    best = jnp.maximum(best, -2.0)
    spread = iota((blocks, total), 0) == numbers[0:1, :]
    inner = ones_where(iota((BLOCK, total), 0) == numbers[1:2, :])
    filled = mm_nt(ones_where(spread), inner)
    result = jnp.zeros((blocks, BLOCK), F32)
    rest = best
    for _ in range(3):
        piece = rest.astype(BF16).astype(F32)
        rest = rest - piece
        result += mm_nt(jnp.where(spread, piece, 0.0).astype(BF16), inner)
    return jnp.where(filled > 0.5, result, -2.0)


def first_score_kernel(blocks, feat, own_ref, next_ref, twin_ref, far_ref, back_ref, right_ref, left_ref, out_ref, bias_ref):
    size = feat + PAY_META
    paired = own_ref[pl.ds(UNITS * size, PAY_META), :].astype(F32) + far_ref[pl.ds(UNITS * size, PAY_META), :].astype(F32)
    penalty = jnp.where(paired > 0.5, 0.0, -4.0).astype(BF16)
    across = [(left_ref, 0), (right_ref, 0), (left_ref, size), (right_ref, size)]
    marks = stack_numbers(across, feat)[0:1, :]
    odd = lax.axis_index("owner") & 1
    marks += 2 * blocks * jnp.where((iota(marks.shape, 1) & BLOCK) == 0, 1 - odd, odd)
    across_bias = bias_of(penalty, marks)
    bias_ref[...] = across_bias
    across_rows = stack_rows(across, feat)
    inside = [(far_ref, size), (next_ref, 0), (back_ref, size), (own_ref, 0), (own_ref, size), (far_ref, size)]
    inside_bias = bias_of(penalty, stack_numbers(inside, feat)[0:1, :] + blocks)
    inside_rows = stack_rows(inside, feat)
    row, lane = iota((4 * BLOCK, 2 * BLOCK), 0), iota((4 * BLOCK, 2 * BLOCK), 1)
    same = jnp.logical_and(row - 3 * BLOCK == lane, lane < BLOCK)
    groups = [
        ([(own_ref, 0), (twin_ref, 0)], 4, 0, 2, None),
        ([(own_ref, size), (far_ref, size)], 2, 1, 5, same),
        ([(back_ref, 0), (next_ref, 0)], 4, 4, 6, None),
    ]
    best, numbers = [], []
    for places, count, low, high, equal in groups:
        part = slice(low * BLOCK, high * BLOCK)
        outer = slice(0, count * BLOCK)
        one = best_of(across_rows[outer], across_bias[outer], places, feat, blocks)
        two = best_of(inside_rows[part], inside_bias[part], places, feat, blocks, equal)
        best.append(jnp.maximum(one, two))
        numbers.append(stack_numbers(places, feat))
    out_ref[...] = slot_table(jnp.concatenate(best, axis=1), jnp.concatenate(numbers, axis=1), blocks)


def second_score_kernel(blocks, feat, table_ref, bias_ref, left_ref, right_ref, back_ref, far_ref, late_ref, out_ref):
    size = feat + PAY_META
    across_rows = stack_rows([(left_ref, 0), (right_ref, 0), (left_ref, size), (right_ref, size)], feat)
    across_bias = bias_ref[...]
    best, numbers = [], []
    for places, count in (([(back_ref, size), (late_ref, 0)], 2), ([(far_ref, 0), (late_ref, size)], 4)):
        outer = slice(0, count * BLOCK)
        best.append(best_of(across_rows[outer], across_bias[outer], places, feat, blocks))
        numbers.append(stack_numbers(places, feat))
    table = slot_table(jnp.concatenate(best, axis=1), jnp.concatenate(numbers, axis=1), blocks)
    table = jnp.maximum(table_ref[...], table)
    for b in range(blocks):
        out_ref[b] = jnp.broadcast_to(table[b : b + 1, :], (8, BLOCK))


def vmem():
    return pl.BlockSpec(memory_space=pltpu.VMEM)


def far():
    return pl.BlockSpec(memory_space=pltpu.HBM)


PARAMS = pltpu.CompilerParams(vmem_limit_bytes=48 * 1024 * 1024)


def cost(flops, nbytes):
    return pl.CostEstimate(flops=flops, bytes_accessed=nbytes, transcendentals=0)


def on_device(embeddings, cluster_of, cluster_owner, slot_of, pairs):
    n_owner = lax.axis_size("owner")
    n_group = lax.axis_size("group")
    rows, feat = embeddings.shape
    chunks = feat // LANES
    cap = 3 * rows // (2 * n_owner * n_group)
    lines = UNITS * cap
    pieces = 2
    size = feat + PAY_META
    outgoing = pl.pallas_call(
        lambda *refs: send_kernel(n_owner, n_group, cap, 6, pieces, *refs),
        out_shape=jax.ShapeDtypeStruct((n_owner, lines * chunks + META, LANES), BF16),
        in_specs=[far()] * 4,
        out_specs=vmem(),
        scratch_shapes=[
            pltpu.VMEM((rows, feat), BF16),
            pltpu.VMEM((n_owner * lines * chunks, LANES), F32),
            pltpu.VMEM((1, rows), I32),
            pltpu.VMEM((1, n_owner), I32),
            pltpu.VMEM((1, rows), I32),
            pltpu.SemaphoreType.DMA((pieces + 3,)),
        ],
        compiler_params=PARAMS,
        name="send_rows",
    )(
        *[
            pltpu.with_memory_space_constraint(x, pltpu.HBM)
            for x in (cluster_of.reshape(1, rows), cluster_owner.reshape(1, n_owner), slot_of.reshape(1, rows), embeddings)
        ]
    )
    arrived = lax.all_to_all(outgoing, "owner", split_axis=0, concat_axis=0, tiled=True)
    swap = [(i, i ^ 1) for i in range(n_group)]

    def along_y(x, partner):
        return lax.ppermute(x, "group", [(i, 2 * (partner(i // 2) % (n_group // 2)) + i % 2) for i in range(n_group)])

    def along_owner(x, partner):
        return lax.ppermute(x, "owner", [(i, partner(i) % n_owner) for i in range(n_owner)])

    entries = pairs.reshape(-1, 2)
    listed = jnp.pad(entries.T, ((0, 0), (0, LANES - entries.shape[0])), constant_values=-1)
    here = pl.pallas_call(
        lambda *refs: list_kernel(n_group, *refs),
        out_shape=jax.ShapeDtypeStruct((n_group, LANES), F32),
        in_specs=[vmem()],
        out_specs=vmem(),
        compiler_params=PARAMS,
        name="list_table",
    )(listed)
    there = along_y(here, lambda y: y ^ 1)
    here = here + there
    there = along_y(here, lambda y: y ^ 2)
    here = here + there
    there = along_y(here, lambda y: y ^ 4)
    both, first = pl.pallas_call(
        lambda *refs: receive_kernel(n_owner, cap, feat, *refs),
        out_shape=[
            jax.ShapeDtypeStruct((UNITS * size + PAY_META, LANES), BF16),
            jax.ShapeDtypeStruct((size, LANES), BF16),
        ],
        in_specs=[vmem()] * 3,
        out_specs=[vmem()] * 2,
        scratch_shapes=[pltpu.VMEM((n_owner * lines * chunks, LANES), F32)],
        compiler_params=PARAMS,
        name="unit_rows",
    )(arrived, here, there)
    back, following = along_y(both, lambda y: y + 1), along_y(first, lambda y: y - 1)
    left, right = along_owner(both, lambda o: o ^ 1), along_owner(both, lambda o: o + 2 * (o & 1) - 1)
    twin = lax.ppermute(both[:size], "group", swap)
    wing = lax.ppermute(jnp.concatenate([back[:size], both[size : 2 * size + PAY_META]], axis=0), "group", swap)
    late = lax.ppermute(jnp.concatenate([back[size : 2 * size], following[:size]], axis=0), "group", swap)
    table, bias = pl.pallas_call(
        lambda *refs: first_score_kernel(n_group, feat, *refs),
        out_shape=[
            jax.ShapeDtypeStruct((n_group, BLOCK), F32),
            jax.ShapeDtypeStruct((4 * BLOCK, n_group), BF16),
        ],
        in_specs=[vmem()] * 7,
        out_specs=[vmem()] * 2,
        compiler_params=PARAMS,
        cost_estimate=cost(3 * 10**9, 4 * 10**6),
        name="score_rows",
    )(both, following, twin, wing, back, right, left)
    table = pl.pallas_call(
        lambda *refs: second_score_kernel(n_group, feat, *refs),
        out_shape=jax.ShapeDtypeStruct((n_group, 8, BLOCK), F32),
        in_specs=[vmem()] * 7,
        out_specs=vmem(),
        compiler_params=PARAMS,
        cost_estimate=cost(5 * 10**8, 2 * 10**6),
        name="score_rest",
    )(table, bias, left, right, back, wing, late)
    shares = lax.all_to_all(table, "group", split_axis=0, concat_axis=0, tiled=True)
    return jnp.max(shares[:, :1], axis=0)


def solution(mesh):
    placed = (P("owner", None), P("owner"), P(), P("owner"), P("owner", "group", None, None))
    return jax.shard_map(
        on_device, mesh=mesh, in_specs=placed, out_specs=P("owner", "group"), check_vma=False
    )
```

```python
import jax
import jax.numpy as jnp
from jax import lax
from jax.experimental import pallas as pl
from jax.experimental.pallas import tpu as pltpu
from jax.sharding import PartitionSpec as P

BLOCK = 128
LANES = 128
META = 8
PAY_META = 16
UNITS = 2
BF16 = jnp.bfloat16
F32 = jnp.float32
I32 = jnp.int32


def iota(shape, dim):
    return lax.broadcasted_iota(I32, shape, dim)


def ones_where(mask):
    return jnp.where(mask, 1.0, 0.0).astype(BF16)


def mm(a, b):
    return jnp.dot(a, b, preferred_element_type=F32)


def mm_nt(a, b):
    return lax.dot_general(a, b, (((1,), (1,)), ((), ())), preferred_element_type=F32)


def mm_tn(a, b):
    return lax.dot_general(a, b, (((0,), (0,)), ((), ())), preferred_element_type=F32)


def send_kernel(n_owner, n_group, cap, shift, pieces, cluster_hbm, owner_hbm, slot_hbm, emb_ref, out_ref, emb, wide, cluster_ref, owner_ref, slot_ref, sems):
    rows, feat = emb.shape
    chunks = feat // LANES
    step = rows // pieces
    small = [
        pltpu.make_async_copy(source, goal, sems.at[pieces + i])
        for i, (source, goal) in enumerate(
            ((cluster_hbm, cluster_ref), (owner_hbm, owner_ref), (slot_hbm, slot_ref))
        )
    ]
    copies = [
        pltpu.make_async_copy(emb_ref.at[pl.ds(i * step, step)], emb.at[pl.ds(i * step, step)], sems.at[i])
        for i in range(pieces)
    ]
    for copy in small + copies:
        copy.start()
    for copy in small:
        copy.wait()
    me = lax.axis_index("group")
    picked = ones_where(iota((n_owner, rows), 0) == cluster_ref[...])
    table = ones_where(iota((n_owner, n_owner), 0) == owner_ref[...])
    to = mm(table, picked).astype(BF16)
    parts = rows // LANES
    stacked = jnp.concatenate([to[:, i * LANES : (i + 1) * LANES] for i in range(parts)], axis=0)
    before = mm(stacked, ones_where(iota((LANES, LANES), 0) < iota((LANES, LANES), 1)))
    totals = mm(stacked, jnp.ones((LANES, LANES), BF16))
    running = jnp.zeros((n_owner, LANES), F32)
    lane_owner = iota((n_owner, LANES), 0).astype(F32)
    place, target = [], []
    for i in range(parts):
        here = stacked[i * n_owner : (i + 1) * n_owner].astype(F32)
        spot = before[i * n_owner : (i + 1) * n_owner] + running
        place.append(jnp.sum(here * spot, axis=0, keepdims=True))
        target.append(jnp.sum(here * lane_owner, axis=0, keepdims=True))
        running = running + totals[i * n_owner : (i + 1) * n_owner]
    place = jnp.concatenate(place, axis=1).astype(I32)
    target = jnp.concatenate(target, axis=1).astype(I32)
    share = place & (n_group - 1)
    entry = place // n_group
    entry = jnp.where(share == me, entry, jnp.where(share == ((me + shift) & (n_group - 1)), entry + cap, -1))
    mine = entry >= 0
    lines = UNITS * cap
    goal = jnp.where(mine, target * lines + entry, -1)
    slot = slot_ref[...]
    high = (slot // BLOCK + 1).astype(F32)
    low = (slot & (BLOCK - 1)).astype(F32)
    width = 16
    row = iota((2 * width, rows), 0)
    values = jnp.where((row & (width - 1)) == entry, jnp.where(row < width, high, low), 0.0).astype(BF16)
    meta = mm_nt(to, values).astype(BF16)
    line = iota((n_owner * META, n_owner), 0)
    peer = iota((n_owner * META, n_owner), 1)
    meta = mm(ones_where(line // META == peer), meta)
    line = iota((n_owner * META, 2 * width), 0) & (META - 1)
    meta = jnp.where(iota((n_owner * META, 2 * width), 1) // width == line, meta, 0.0).astype(BF16)
    column = iota((2 * width, LANES), 0) & (width - 1)
    meta = mm(meta, ones_where(column == iota((2 * width, LANES), 1)))
    out_ref[:, lines * chunks :, :] = meta.reshape(n_owner, META, LANES).astype(BF16)
    middle = n_owner * lines // 2
    line = (iota((n_owner * lines, 1), 0) - middle).astype(F32).astype(BF16)
    goal = jnp.where(mine, goal - middle, middle).astype(F32).astype(BF16)
    select = jnp.where(line == goal, jnp.ones((), BF16), jnp.zeros((), BF16))
    total = None
    for i, copy in enumerate(copies[:-1]):
        copy.wait()
        part = mm(select[:, i * step : (i + 1) * step], emb[pl.ds(i * step, step), :])
        total = part if total is None else total + part
    copies[-1].wait()
    last = rows - step
    for k in range(0, chunks, 2):
        part = total[:, k * LANES : (k + 2) * LANES]
        part += mm(select[:, last:], emb[pl.ds(last, step), pl.ds(k * LANES, 2 * LANES)])
        for h in range(2):
            wide[pl.ds(k + h, n_owner * lines, chunks), :] = part[:, h * LANES : (h + 1) * LANES]
    out_ref[:, : lines * chunks, :] = wide[...].reshape(n_owner, lines * chunks, LANES).astype(BF16)


def list_kernel(blocks, pairs_ref, out_ref):
    first, second = pairs_ref[0:1, :], pairs_ref[1:2, :]
    rows, wide = iota((blocks, LANES), 0), iota((LANES, LANES), 0)
    table = mm_nt(ones_where(rows == first), ones_where(wide == second))
    out_ref[...] = table + mm_nt(ones_where(rows == second - blocks), ones_where(wide == first + blocks))


def receive_kernel(n_owner, cap, feat, in_ref, here_ref, there_ref, both_ref, first_ref, wide):
    chunks = feat // LANES
    per_peer = UNITS * cap
    lines = n_owner * per_peer
    size = feat + PAY_META
    wide[...] = in_ref[:, : per_peer * chunks, :].astype(F32).reshape(lines * chunks, LANES)
    meta = in_ref[:, per_peer * chunks :, :].astype(F32).reshape(n_owner * META, LANES).astype(BF16)
    line = iota((lines, n_owner * META), 0)
    source = iota((lines, n_owner * META), 1)
    at_lane = iota((lines, LANES), 1) == lax.rem(iota((lines, LANES), 0), per_peer)
    high = mm(ones_where(source == line // per_peer * META), meta)
    low = mm(ones_where(source == line // per_peer * META + 1), meta)
    ones = jnp.ones((LANES, LANES), BF16)
    high = mm(jnp.where(at_lane, high, 0.0).astype(BF16), ones)
    low = mm(jnp.where(at_lane, low, 0.0).astype(BF16), ones)
    valid = ones_where(high > 0.5)
    later, sooner = iota((lines, lines), 0), iota((lines, lines), 1)
    same = lax.rem(later, per_peer) // cap == lax.rem(sooner, per_peer) // cap
    place = mm(ones_where(jnp.logical_and(sooner < later, same)), valid)
    unit = lax.rem(iota((lines, BLOCK), 0), per_peer) // cap
    here = jnp.logical_and(place == iota((lines, BLOCK), 1).astype(F32), high > 0.5)
    puts = [jnp.logical_and(here, unit == n) for n in range(UNITS)]
    put_one = ones_where(jnp.concatenate(puts, axis=1))
    parts = []
    square = None
    for k in range(chunks):
        part = mm_tn(put_one, wide[pl.ds(k, lines, chunks), :].astype(BF16))
        parts.append(part)
        here = part * part
        square = here if square is None else square + here
    scale = lax.rsqrt(jnp.sum(square, axis=1, keepdims=True) + 1e-06)
    for k in range(chunks):
        piece = (parts[k] * scale).astype(BF16)
        for n in range(UNITS):
            both_ref[pl.ds(n * size + k * BLOCK, BLOCK), :] = piece[n * BLOCK : (n + 1) * BLOCK]
        first_ref[pl.ds(k * BLOCK, BLOCK), :] = piece[:BLOCK]
    row = iota((PAY_META, LANES), 0)
    for n in range(UNITS):
        blocks = jnp.sum(jnp.where(puts[n], high, 0.0), axis=0, keepdims=True) - 1.0
        inner = jnp.sum(jnp.where(puts[n], low, 0.0), axis=0, keepdims=True)
        numbers = jnp.where(row == 0, blocks, jnp.where(row == 1, inner, 0.0)).astype(BF16)
        both_ref[pl.ds(n * size + feat, PAY_META), :] = numbers
        if n == 0:
            first_ref[pl.ds(feat, PAY_META), :] = numbers
    both_ref[pl.ds(UNITS * size, PAY_META), :] = (here_ref[...] + there_ref[...]).astype(BF16)


def rows_of(ref, start, feat):
    return jnp.concatenate([ref[pl.ds(start + k * BLOCK, BLOCK), :] for k in range(feat // LANES)], axis=1)


def numbers_of(ref, start, feat):
    return ref[pl.ds(start + feat, PAY_META), :].astype(F32)[0:2, :].astype(I32)


def stack_rows(places, feat):
    return jnp.concatenate([rows_of(ref, start, feat) for ref, start in places], axis=0)


def stack_numbers(places, feat):
    return jnp.concatenate([numbers_of(ref, start, feat) for ref, start in places], axis=1)


def best_of(left, bias, places, feat, blocks, same=None):
    right = stack_rows(places, feat)
    width = right.shape[0]
    here = ones_where(iota((blocks, width), 0) == stack_numbers(places, feat)[0:1, :])
    scores = mm_nt(left, right) + mm(bias, here)
    if same is not None:
        scores = jnp.where(same, -2.0, scores)
    return jnp.max(scores, axis=0, keepdims=True)


def bias_of(penalty, marks):
    picked = ones_where(iota((LANES, marks.shape[1]), 0) == marks)
    return lax.dot_general(picked, penalty, (((0,), (1,)), ((), ())), preferred_element_type=F32).astype(BF16)


def slot_table(best, numbers, blocks):
    total = best.shape[1]
    best = jnp.maximum(best, -2.0)
    spread = iota((blocks, total), 0) == numbers[0:1, :]
    inner = ones_where(iota((BLOCK, total), 0) == numbers[1:2, :])
    filled = mm_nt(ones_where(spread), inner)
    result = jnp.zeros((blocks, BLOCK), F32)
    rest = best
    for _ in range(3):
        piece = rest.astype(BF16).astype(F32)
        rest = rest - piece
        result += mm_nt(jnp.where(spread, piece, 0.0).astype(BF16), inner)
    return jnp.where(filled > 0.5, result, -2.0)


def first_score_kernel(blocks, feat, own_ref, next_ref, twin_ref, far_ref, back_ref, right_ref, left_ref, out_ref, bias_ref):
    size = feat + PAY_META
    paired = own_ref[pl.ds(UNITS * size, PAY_META), :].astype(F32) + far_ref[pl.ds(UNITS * size, PAY_META), :].astype(F32)
    penalty = jnp.where(paired > 0.5, 0.0, -4.0).astype(BF16)
    across = [(left_ref, 0), (right_ref, 0), (left_ref, size), (right_ref, size)]
    marks = stack_numbers(across, feat)[0:1, :]
    odd = lax.axis_index("owner") & 1
    marks += 2 * blocks * jnp.where((iota(marks.shape, 1) & BLOCK) == 0, 1 - odd, odd)
    across_bias = bias_of(penalty, marks)
    bias_ref[...] = across_bias
    across_rows = stack_rows(across, feat)
    inside = [(far_ref, size), (next_ref, 0), (back_ref, size), (own_ref, 0), (own_ref, size), (far_ref, size)]
    inside_bias = bias_of(penalty, stack_numbers(inside, feat)[0:1, :] + blocks)
    inside_rows = stack_rows(inside, feat)
    row, lane = iota((4 * BLOCK, 2 * BLOCK), 0), iota((4 * BLOCK, 2 * BLOCK), 1)
    same = jnp.logical_and(row - 3 * BLOCK == lane, lane < BLOCK)
    groups = [
        ([(own_ref, 0), (twin_ref, 0)], 4, 0, 2, None),
        ([(own_ref, size), (far_ref, size)], 2, 1, 5, same),
        ([(back_ref, 0), (next_ref, 0)], 4, 4, 6, None),
    ]
    wide = best_of(across_rows, across_bias, groups[0][0] + groups[2][0], feat, blocks)
    near = best_of(across_rows[: 2 * BLOCK], across_bias[: 2 * BLOCK], groups[1][0], feat, blocks)
    outer = [wide[:, : 2 * BLOCK], near, wide[:, 2 * BLOCK :]]
    best, numbers = [], []
    for one, (places, _, low, high, equal) in zip(outer, groups):
        part = slice(low * BLOCK, high * BLOCK)
        two = best_of(inside_rows[part], inside_bias[part], places, feat, blocks, equal)
        best.append(jnp.maximum(one, two))
        numbers.append(stack_numbers(places, feat))
    out_ref[...] = slot_table(jnp.concatenate(best, axis=1), jnp.concatenate(numbers, axis=1), blocks)


def second_score_kernel(blocks, feat, table_ref, bias_ref, left_ref, right_ref, back_ref, far_ref, late_ref, out_ref):
    size = feat + PAY_META
    across_rows = stack_rows([(left_ref, 0), (right_ref, 0), (left_ref, size), (right_ref, size)], feat)
    across_bias = bias_ref[...]
    best, numbers = [], []
    for places, count in (([(back_ref, size), (late_ref, 0)], 2), ([(far_ref, 0), (late_ref, size)], 4)):
        outer = slice(0, count * BLOCK)
        best.append(best_of(across_rows[outer], across_bias[outer], places, feat, blocks))
        numbers.append(stack_numbers(places, feat))
    table = slot_table(jnp.concatenate(best, axis=1), jnp.concatenate(numbers, axis=1), blocks)
    table = jnp.maximum(table_ref[...], table)
    for b in range(blocks):
        out_ref[b] = jnp.broadcast_to(table[b : b + 1, :], (8, BLOCK))


def vmem():
    return pl.BlockSpec(memory_space=pltpu.VMEM)


def far():
    return pl.BlockSpec(memory_space=pltpu.HBM)


PARAMS = pltpu.CompilerParams(vmem_limit_bytes=48 * 1024 * 1024)


def cost(flops, nbytes):
    return pl.CostEstimate(flops=flops, bytes_accessed=nbytes, transcendentals=0)


def on_device(embeddings, cluster_of, cluster_owner, slot_of, pairs):
    n_owner = lax.axis_size("owner")
    n_group = lax.axis_size("group")
    rows, feat = embeddings.shape
    chunks = feat // LANES
    cap = 3 * rows // (2 * n_owner * n_group)
    lines = UNITS * cap
    pieces = 2
    size = feat + PAY_META
    outgoing = pl.pallas_call(
        lambda *refs: send_kernel(n_owner, n_group, cap, 6, pieces, *refs),
        out_shape=jax.ShapeDtypeStruct((n_owner, lines * chunks + META, LANES), BF16),
        in_specs=[far()] * 4,
        out_specs=vmem(),
        scratch_shapes=[
            pltpu.VMEM((rows, feat), BF16),
            pltpu.VMEM((n_owner * lines * chunks, LANES), F32),
            pltpu.VMEM((1, rows), I32),
            pltpu.VMEM((1, n_owner), I32),
            pltpu.VMEM((1, rows), I32),
            pltpu.SemaphoreType.DMA((pieces + 3,)),
        ],
        compiler_params=PARAMS,
        name="send_rows",
    )(
        *[
            pltpu.with_memory_space_constraint(x, pltpu.HBM)
            for x in (cluster_of.reshape(1, rows), cluster_owner.reshape(1, n_owner), slot_of.reshape(1, rows), embeddings)
        ]
    )
    arrived = lax.all_to_all(outgoing, "owner", split_axis=0, concat_axis=0, tiled=True)
    swap = [(i, i ^ 1) for i in range(n_group)]

    def along_y(x, partner):
        return lax.ppermute(x, "group", [(i, 2 * (partner(i // 2) % (n_group // 2)) + i % 2) for i in range(n_group)])

    def along_owner(x, partner):
        return lax.ppermute(x, "owner", [(i, partner(i) % n_owner) for i in range(n_owner)])

    entries = pairs.reshape(-1, 2)
    listed = jnp.pad(entries.T, ((0, 0), (0, LANES - entries.shape[0])), constant_values=-1)
    here = pl.pallas_call(
        lambda *refs: list_kernel(n_group, *refs),
        out_shape=jax.ShapeDtypeStruct((n_group, LANES), F32),
        in_specs=[vmem()],
        out_specs=vmem(),
        compiler_params=PARAMS,
        name="list_table",
    )(listed)
    there = along_y(here, lambda y: y ^ 1)
    here = here + there
    there = along_y(here, lambda y: y ^ 2)
    here = here + there
    there = along_y(here, lambda y: y ^ 4)
    both, first = pl.pallas_call(
        lambda *refs: receive_kernel(n_owner, cap, feat, *refs),
        out_shape=[
            jax.ShapeDtypeStruct((UNITS * size + PAY_META, LANES), BF16),
            jax.ShapeDtypeStruct((size, LANES), BF16),
        ],
        in_specs=[vmem()] * 3,
        out_specs=[vmem()] * 2,
        scratch_shapes=[pltpu.VMEM((n_owner * lines * chunks, LANES), F32)],
        compiler_params=PARAMS,
        name="unit_rows",
    )(arrived, here, there)
    back, following = along_y(both, lambda y: y + 1), along_y(first, lambda y: y - 1)
    left, right = along_owner(both, lambda o: o ^ 1), along_owner(both, lambda o: o + 2 * (o & 1) - 1)
    twin = lax.ppermute(both[:size], "group", swap)
    wing = lax.ppermute(jnp.concatenate([back[:size], both[size : 2 * size + PAY_META]], axis=0), "group", swap)
    late = lax.ppermute(jnp.concatenate([back[size : 2 * size], following[:size]], axis=0), "group", swap)
    table, bias = pl.pallas_call(
        lambda *refs: first_score_kernel(n_group, feat, *refs),
        out_shape=[
            jax.ShapeDtypeStruct((n_group, BLOCK), F32),
            jax.ShapeDtypeStruct((4 * BLOCK, n_group), BF16),
        ],
        in_specs=[vmem()] * 7,
        out_specs=[vmem()] * 2,
        compiler_params=PARAMS,
        cost_estimate=cost(3 * 10**9, 4 * 10**6),
        name="score_rows",
    )(both, following, twin, wing, back, right, left)
    table = pl.pallas_call(
        lambda *refs: second_score_kernel(n_group, feat, *refs),
        out_shape=jax.ShapeDtypeStruct((n_group, 8, BLOCK), F32),
        in_specs=[vmem()] * 7,
        out_specs=vmem(),
        compiler_params=PARAMS,
        cost_estimate=cost(5 * 10**8, 2 * 10**6),
        name="score_rest",
    )(table, bias, left, right, back, wing, late)
    shares = lax.all_to_all(table, "group", split_axis=0, concat_axis=0, tiled=True)
    return jnp.max(shares, axis=(0, 1)).reshape(1, LANES)


def solution(mesh):
    placed = (P("owner", None), P("owner"), P(), P("owner"), P("owner", "group", None, None))
    return jax.shard_map(
        on_device, mesh=mesh, in_specs=placed, out_specs=P("owner", "group"), check_vma=False
    )
```
